32 devices in a mesh: grp: 2 (over y), seg: 4 (over z), tok: 4 (over x, core).
Axes of the slice: x: 2, y: 2, z: 4, core: 2. Of those that a mesh axis runs over, the one named last changes fastest.
Arguments:
- hidden_in: bfloat16 [4, 4096, 2048], P('grp', ('seg', 'tok')), may hold values from -6 to 6
- cotangent: bfloat16 [4, 4096, 2048], P('grp', ('seg', 'tok')), may hold values from -6 to 6
- piece_start: int32 [4, 4], P('grp', 'seg'), may hold values from 0 to 3840, as said below
- query_weight: bfloat16 [2048, 2048], P('seg', 'tok'), may hold values from -0.125 to 0.125
- key_weight: bfloat16 [2048, 2048], P('seg', 'tok'), may hold values from -0.125 to 0.125
- value_weight: bfloat16 [2048, 2048], P('seg', 'tok'), may hold values from -0.125 to 0.125
- out_weight: bfloat16 [2048, 2048], P('seg', 'tok'), may hold values from -0.375 to 0.375
- gate_weight: bfloat16 [2048, 8192], P('seg', 'tok'), may hold values from -0.125 to 0.125
- up_weight: bfloat16 [2048, 8192], P('seg', 'tok'), may hold values from -0.125 to 0.125
- down_weight: bfloat16 [2048, 8192], P('seg', 'tok'), may hold values from -0.0625 to 0.0625
- attend_gain: float32 [2048], replicated, may hold values from 0.5 to 1.5
- feed_gain: float32 [2048], replicated, may hold values from 0.5 to 1.5
- gate_logit: float32 [16], replicated, may hold values from -2 to 2
Outputs:
- output: bfloat16 [4, 4096, 2048], P('grp', ('seg', 'tok'))
- input_grad: bfloat16 [4, 4096, 2048], P('grp', ('seg', 'tok'))
- query_grad: float32 [2048, 2048], P('seg', 'tok')
- key_grad: float32 [2048, 2048], P('seg', 'tok')
- value_grad: float32 [2048, 2048], P('seg', 'tok')
- out_grad: float32 [2048, 2048], P('seg', 'tok')
- gate_grad: float32 [2048, 8192], P('seg', 'tok')
- up_grad: float32 [2048, 8192], P('seg', 'tok')
- down_grad: float32 [2048, 8192], P('seg', 'tok')
- attend_gain_grad: float32 [2048], replicated
- feed_gain_grad: float32 [2048], replicated
- gate_logit_grad: float32 [16], replicated
The draws below stay inside these ranges and needn't reach their ends.
Inputs may be any that keep to these rules, and one draw needn't show every extreme that they name: `piece_start`: entry k of a sequence's row is the first position of that sequence's one picture piece of segment k; its 256 positions lie inside positions k * 1024 to (k + 1) * 1024 - 1.
All inputs are finite; a program needn't handle non-finite values.
Results may differ from the reference program's by a relative error of at most 0.02.
Values may be sent and summed in bfloat16 or wider, within the bound.
No kernel may reach another device: no remote copies, remote signals or barrier semaphores. Data moves between devices by JAX's collectives and lax.ppermute only.
A program may use at most 384 MiB of HBM per device.

```python
import jax
import jax.numpy as jnp
from jax import lax

D = 2048
HEADS = 16
HEAD_DIM = 128
FF = 8192
SEG_LEN = 1024
PIECE = 256
SEQS = 4
SEGS = 4
LENGTH = 4096


def draw_piece_start(key, part):
    offsets = jax.random.randint(key, (SEQS, SEGS), 0, SEG_LEN - PIECE + 1, dtype=jnp.int32)
    return offsets + (jnp.arange(SEGS, dtype=jnp.int32) * SEG_LEN)[None, :]


def level_of(key, dims, cuts, least, largest):
    loudness, own = 1.0, jax.random.fold_in(key, 6)
    for dim, blocks in cuts:
        draws = jnp.exp(jax.random.uniform(jax.random.fold_in(own, dim), (blocks,), jnp.float32, least / len(cuts), largest / len(cuts)))
        loudness = loudness * jnp.repeat(draws, dims[dim] // blocks).reshape([-1 if axis == dim else 1 for axis in range(len(dims))])
    return loudness


def gaussian(own_key, dims, scale, most, cuts=(), held_as=jnp.bfloat16):
    values = jax.random.normal(own_key, dims, jnp.float32) * scale
    if len(cuts) > 0:
        values = level_of(own_key, dims, cuts, -0.22, 0.18) * values
    return jnp.clip(values, min=-most, max=most).astype(held_as)


def setup_inputs(seed: int = 0) -> dict:
    key_of = jax.random.split(jax.random.key(seed), 14)
    return {
        "hidden_in": gaussian(key_of[0], (SEQS, LENGTH, D), 1.0, 6.0, ((0, 2), (1, 16))),
        "cotangent": gaussian(key_of[1], (SEQS, LENGTH, D), 1.0, 6.0, ((0, 2), (1, 16))),
        "piece_start": draw_piece_start(jax.random.fold_in(key_of[13], 71), 0),
        "query_weight": gaussian(key_of[3], (D, HEADS * HEAD_DIM), D ** -0.5, 0.125, ((0, 4), (1, 4))),
        "key_weight": gaussian(key_of[4], (D, HEADS * HEAD_DIM), D ** -0.5, 0.125, ((0, 4), (1, 4))),
        "value_weight": gaussian(key_of[5], (D, HEADS * HEAD_DIM), D ** -0.5, 0.125, ((0, 4), (1, 4))),
        "out_weight": gaussian(key_of[6], (D, HEADS * HEAD_DIM), (HEADS * HEAD_DIM // 8) ** -0.5, 0.375, ((0, 4), (1, 4))),
        "gate_weight": gaussian(key_of[7], (D, FF), D ** -0.5, 0.125, ((0, 4), (1, 4))),
        "up_weight": gaussian(key_of[8], (D, FF), D ** -0.5, 0.125, ((0, 4), (1, 4))),
        "down_weight": gaussian(key_of[9], (D, FF), FF ** -0.5, 0.0625, ((0, 4), (1, 4))),
        "attend_gain": jnp.clip(1.0 + 0.1 * jax.random.normal(key_of[10], (D,), jnp.float32), 0.5, 1.5),
        "feed_gain": jnp.clip(1.0 + 0.1 * jax.random.normal(key_of[11], (D,), jnp.float32), 0.5, 1.5),
        "gate_logit": jnp.clip(jax.random.uniform(key_of[12], (HEADS,), jnp.float32, -2.0, 2.0), -2.0, 2.0),
    }


EPS_NORM = 1e-05
MASKED_SCORE = -1e+30

@jax.custom_vjp
def low(v):
    return lax.optimization_barrier(v.astype(jnp.bfloat16)).astype(jnp.float32)

@jax.custom_vjp
def low_back(v):
    return v

def low_keep(v):
    return (low(v), None)

def low_pass(kept, grad):
    return (grad,)

def back_keep(v):
    return (v, None)

def back_low(kept, grad):
    return (low(grad),)
low.defvjp(low_keep, low_pass)
low_back.defvjp(back_keep, back_low)

def matmul_high(left_side, right_side):
    return jnp.dot(left_side, right_side, precision=lax.Precision.HIGHEST)

def root_norm(values, gain):
    return values * lax.rsqrt(lax.optimization_barrier(jnp.mean(values * values, -1, keepdims=True)) + EPS_NORM) * gain

def positive_feature(values):
    return jnp.where(values > 0, values + 1.0, jnp.exp(jnp.where(values > 0, 0.0, values)))

def segment_attend(items):
    queries, key_rows, values, piece_first = items
    rows_at = jnp.arange(SEG_LEN, dtype=jnp.int32)[:, None]
    keys_at = jnp.arange(SEG_LEN, dtype=jnp.int32)[None, :]
    row_in = (rows_at >= piece_first) & (rows_at < piece_first + PIECE)
    key_in = (keys_at >= piece_first) & (keys_at < piece_first + PIECE)
    visible = (keys_at <= rows_at) | row_in & key_in
    scores = low_back(jnp.einsum('qhd,khd->hqk', queries, key_rows, precision=lax.Precision.HIGHEST) * HEAD_DIM ** (-0.5))
    scores = jnp.where(visible[None], scores, MASKED_SCORE)
    probs = jax.nn.softmax(scores, axis=-1)
    return low_back(jnp.einsum('hqk,khd->qhd', low(probs), values, precision=lax.Precision.HIGHEST))

def exclusive_prefix(stacked):
    return jnp.concatenate([jnp.zeros_like(stacked[:1]), jnp.cumsum(stacked[:-1], axis=0)], axis=0)

def forward(hidden, weights, piece_row):
    query_weight, key_weight, value_weight, out_weight, gate_weight, up_weight, down_weight, attend_gain, feed_gain, gate_logit = weights
    head_shape = (SEGS, SEG_LEN, HEADS, HEAD_DIM)
    normed_a = low(root_norm(hidden, attend_gain))
    queries = low(low_back(matmul_high(normed_a, query_weight))).reshape(head_shape)
    key_rows = low(low_back(matmul_high(normed_a, key_weight))).reshape(head_shape)
    values = low(low_back(matmul_high(normed_a, value_weight))).reshape(head_shape)
    feat_q = low(positive_feature(queries))
    feat_k = low(positive_feature(key_rows))
    contrib = jnp.einsum('sthd,sthe->shde', feat_k, values, precision=lax.Precision.HIGHEST)
    count_k = lax.optimization_barrier(jnp.sum(feat_k, axis=1))
    memory = exclusive_prefix(contrib)
    norm_mem = exclusive_prefix(count_k)
    numerator = low_back(jnp.einsum('sthd,shde->sthe', feat_q, low(memory), precision=lax.Precision.HIGHEST))
    denominator = 1.0 + jnp.einsum('sthd,shd->sth', feat_q, norm_mem, precision=lax.Precision.HIGHEST)[..., None]
    recall = numerator / denominator
    piece_rel = piece_row - jnp.arange(SEGS, dtype=jnp.int32) * SEG_LEN
    local_out = lax.map(jax.checkpoint(segment_attend), (queries, key_rows, values, piece_rel))
    gate_share = jax.nn.sigmoid(gate_logit)[None, None, :, None]
    mixed_out = low(gate_share * recall + (1.0 - gate_share) * local_out).reshape(LENGTH, HEADS * HEAD_DIM)
    attended = low_back(matmul_high(mixed_out, out_weight.T))
    resid = hidden + attended
    normed_f = low(root_norm(resid, feed_gain))
    gate_pre = low_back(matmul_high(normed_f, gate_weight))
    up_pre = low_back(matmul_high(normed_f, up_weight))
    inner_act = low(jax.nn.silu(gate_pre) * up_pre)
    return resid + low_back(matmul_high(inner_act, down_weight.T))

def reference(hidden_in, cotangent, piece_start, query_weight, key_weight, value_weight, out_weight, gate_weight, up_weight, down_weight, attend_gain, feed_gain, gate_logit):
    weights = tuple((item.astype(jnp.float32) for item in (query_weight, key_weight, value_weight, out_weight, gate_weight, up_weight, down_weight, attend_gain, feed_gain, gate_logit)))

    def one_sequence(carry, entries):
        hidden, cot_rows, piece_row = entries
        result, pull = jax.vjp(lambda hidden_v, weight_v: forward(hidden_v, weight_v, piece_row), hidden.astype(jnp.float32), weights)
        grad_hidden, grad_weights = pull(cot_rows.astype(jnp.float32))
        carry = jax.tree.map(jnp.add, carry, grad_weights)
        return (carry, (result.astype(jnp.bfloat16), grad_hidden.astype(jnp.bfloat16)))
    zeros_start = jax.tree.map(jnp.zeros_like, weights)
    grads, (outputs, input_grads) = lax.scan(one_sequence, zeros_start, (hidden_in, cotangent, piece_start))
    return (outputs, input_grads, grads[0], grads[1], grads[2], grads[3], grads[4], grads[5], grads[6], grads[7], grads[8], grads[9])
```

```python
import jax
import jax.numpy as jnp
from jax import lax
from jax.experimental import pallas as pl
from jax.experimental.pallas import tpu as pltpu
from jax.sharding import PartitionSpec as P

HEADS = 16
HEAD_DIM = 128
SEG_LEN = 1024
PIECE = 256
VMEM_BYTES = 60 * 1024 * 1024
MICRO = 2


EPS_NORM = 1e-05
MASKED_SCORE = -1e30


class Line:
    def __init__(self, token):
        self.token = token

    def hold(self, value):
        value, self.token = lax.optimization_barrier((value, self.token))
        return value

    def __call__(self, step, *inputs):
        return self.hold(step(*self.hold(inputs)))


def tok_bits():
    return [1 << k for k in range(lax.axis_size("tok").bit_length() - 1)]


def tok_swap(value, bit):
    count = lax.axis_size("tok")
    return lax.ppermute(value, "tok", [(k, k ^ bit) for k in range(count)])


def tok_at(bit):
    return jnp.where((lax.axis_index("tok") & bit) == 0, 0, 1)


def grp_swap(value):
    return lax.ppermute(value, "grp", [(0, 1), (1, 0)])


def tok_pieces(rows, bits):
    pieces = {0: rows}
    for bit in reversed(bits):
        for at in sorted(pieces):
            pieces[at | bit] = tok_swap(pieces[at], bit)
    return pieces


class FirstPiece:
    def __init__(self, rows, bits):
        self.rows = rows
        self.bits = bits
        self.got = tok_swap(rows, bits[-1])

    def rest(self, line):
        pieces = {0: self.rows, self.bits[-1]: line.hold(self.got)}
        for bit in reversed(self.bits[:-1]):
            for at in sorted(pieces):
                pieces[at | bit] = tok_swap(pieces[at], bit)
        return pieces


def added(kept, got):
    return kept.astype(jnp.float32) + got.astype(jnp.float32)


class Scatter:
    def __init__(self, kept, sent):
        self.bits = tok_bits()
        self.terms = (kept, tok_swap(sent, self.bits[0]))

    def go_on(self, line):
        def cut(*terms):
            half = terms[0].shape[0] // 2
            return sum(term[half:].astype(jnp.float32) for term in terms).astype(jnp.bfloat16)

        for bit in self.bits[1:]:
            got = tok_swap(line(cut, *self.terms), bit)
            half = got.shape[0]
            self.terms = tuple(term[:half] for term in self.terms) + (got,)


def total_of(terms):
    return sum(term.astype(jnp.float32) for term in terms)


def tok_order(bits):
    order = [0]
    for bit in reversed(bits):
        order = order + [at | bit for at in order]
    return order


def kernel_params():
    return pltpu.CompilerParams(vmem_limit_bytes=VMEM_BYTES)


def kernel_cost(flops, *arrays):
    moved = sum(a.size * a.dtype.itemsize for a in arrays)
    return pl.CostEstimate(flops=flops, transcendentals=0, bytes_accessed=moved)


def any_space():
    return pl.BlockSpec(memory_space=pl.ANY)


def kept_block(shape):
    return pl.BlockSpec(shape, lambda *at: (0,) * len(shape), pipeline_mode=pl.Buffered(1))


def place(pieces, spots):
    rows, width = pieces[0].shape[-2:]
    total = sum(p.shape[0] for p in pieces)

    def kernel(spots_ref, *refs):
        *ins, out, held, arrive, leave = refs
        copies = []
        for ref in ins:
            for j in range(ref.shape[0]):
                at = len(copies)
                start = pl.multiple_of(spots_ref[at] * rows, rows)
                copies.append(
                    (
                        pltpu.make_async_copy(ref.at[j], held.at[at], arrive.at[at]),
                        pltpu.make_async_copy(
                            held.at[at], out.at[pl.ds(start, rows)], leave.at[at]
                        ),
                    )
                )
        for first, _ in copies:
            first.start()
        for first, then in copies:
            first.wait()
            then.start()
        for _, then in copies:
            then.wait()

    out = jax.ShapeDtypeStruct((total * rows, width), pieces[0].dtype)
    return pl.pallas_call(
        kernel,
        in_specs=[pl.BlockSpec(memory_space=pltpu.SMEM)] + [any_space()] * len(pieces),
        out_specs=any_space(),
        out_shape=out,
        scratch_shapes=[
            pltpu.VMEM((total, rows, width), pieces[0].dtype),
            pltpu.SemaphoreType.DMA((total,)),
            pltpu.SemaphoreType.DMA((total,)),
        ],
        compiler_params=kernel_params(),
        cost_estimate=kernel_cost(0, out, out),
    )(spots, *pieces)


def over_pieces(pieces, which, extra, extra_specs, outs, compute, flops):
    rows, width = pieces[0].shape[-2:]
    total = rows * len(pieces)
    block = max(rows, min(512, total))
    each = block // rows

    def kernel(*refs):
        ins = refs[: len(pieces)]
        others = refs[len(pieces) : len(pieces) + len(extra)]
        results = refs[len(pieces) + len(extra) : -2]
        held, arrive = refs[-2:]
        step = pl.program_id(0)

        def copy(at, ref):
            return pltpu.make_async_copy(
                ref.at[which], held.at[pl.ds(at * rows, rows)], arrive.at[at]
            )

        @pl.when(step == 0)
        def start_all():
            for at, ref in enumerate(ins):
                copy(at, ref).start()

        for part in range(each):
            copy(step * each + part, ins[0]).wait()
        x = held[pl.ds(pl.multiple_of(step * block, block), block)]
        results[0][...] = x
        compute(x, others, results[1:])

    row_spec = lambda n: pl.BlockSpec((block, n), lambda i: (i, 0))
    shapes = [jax.ShapeDtypeStruct((total, n), jnp.bfloat16) for n in (width,) + tuple(outs)]
    return pl.pallas_call(
        kernel,
        grid=(total // block,),
        in_specs=[any_space()] * len(pieces) + [spec(row_spec) for spec in extra_specs],
        out_specs=[row_spec(s.shape[1]) for s in shapes],
        out_shape=shapes,
        scratch_shapes=[
            pltpu.VMEM((total, width), pieces[0].dtype),
            pltpu.SemaphoreType.DMA((len(pieces),)),
        ],
        compiler_params=kernel_params(),
        cost_estimate=kernel_cost(flops, *shapes, *extra),
    )(*pieces, *extra)


def feed_forward(pieces, which, weight):
    hidden = weight.shape[1] // 2
    total = len(pieces) * pieces[0].shape[-2]

    def compute(x, others, results):
        both = jnp.dot(x, others[0][...], preferred_element_type=jnp.float32)
        gate, up = (both[:, :hidden], both[:, hidden:])
        results[0][...] = both.astype(jnp.bfloat16)
        results[1][...] = (gate * jax.nn.sigmoid(gate) * up).astype(jnp.bfloat16)

    return over_pieces(
        pieces,
        which,
        (weight,),
        (lambda row_spec: kept_block(weight.shape),),
        (2 * hidden, hidden),
        compute,
        2 * total * weight.size,
    )


def feed_backward(pieces, which, weight, both):
    hidden = weight.shape[1]
    total = len(pieces) * pieces[0].shape[-2]

    def compute(x, others, results):
        grad = jnp.dot(x, others[0][...], preferred_element_type=jnp.float32)
        gate = others[1][:, :hidden].astype(jnp.float32)
        up = others[1][:, hidden:].astype(jnp.float32)
        sig = jax.nn.sigmoid(gate)
        results[0][:, :hidden] = (grad * up * sig * (1.0 + gate * (1.0 - sig))).astype(jnp.bfloat16)
        results[0][:, hidden:] = (grad * gate * sig).astype(jnp.bfloat16)

    return over_pieces(
        pieces,
        which,
        (weight, both),
        (lambda row_spec: kept_block(weight.shape), lambda row_spec: row_spec(2 * hidden)),
        (2 * hidden,),
        compute,
        2 * total * weight.size,
    )


def products_cut(lefts, weights, order):
    total, width = (lefts[0].shape[0], weights[0].shape[0])
    steps = order.shape[0]
    rows = total // steps
    half = steps // 2
    pairs = len(lefts)

    def kernel(order_ref, *refs):
        out = 0.0
        for left, weight in zip(refs[:pairs], refs[pairs : 2 * pairs]):
            out = out + lax.dot_general(
                left[...],
                weight[...],
                (((1,), (1,)), ((), ())),
                preferred_element_type=jnp.float32,
            )
        sent_ref, kept_ref = refs[2 * pairs :]
        step = pl.program_id(0)

        @pl.when(step < half)
        def first_part():
            sent_ref[...] = out.astype(jnp.bfloat16)

        @pl.when(step >= half)
        def second_part():
            kept_ref[...] = out.astype(jnp.bfloat16)

    part = jax.ShapeDtypeStruct((total // 2, width), jnp.bfloat16)
    sent, kept = pl.pallas_call(
        kernel,
        grid_spec=pltpu.PrefetchScalarGridSpec(
            num_scalar_prefetch=1,
            grid=(steps,),
            in_specs=[
                pl.BlockSpec(
                    (rows, left.shape[1]), lambda i, at: (at[lax.rem(i + half, steps)], 0)
                )
                for left in lefts
            ]
            + [kept_block(weight.shape) for weight in weights],
            out_specs=[
                pl.BlockSpec((rows, width), lambda i, at: (jnp.minimum(i, half - 1), 0)),
                pl.BlockSpec((rows, width), lambda i, at: (jnp.maximum(i - half, 0), 0)),
            ],
        ),
        out_shape=[part, part],
        compiler_params=kernel_params(),
        cost_estimate=kernel_cost(
            sum(2 * total * weight.size for weight in weights), part, part, *lefts, *weights
        ),
    )(order, *lefts, *weights)
    return (kept, sent)


def grad_product(rows_of, columns_of):
    pairs = len(rows_of)
    total, width = rows_of[0].shape
    columns = columns_of[0].shape[1]
    block = 256

    def kernel(*refs):
        out = 0.0
        for left, right in zip(refs[:pairs], refs[pairs : 2 * pairs]):
            out = out + lax.dot_general(
                left[...],
                right[...],
                (((0,), (0,)), ((), ())),
                preferred_element_type=jnp.float32,
            )
        refs[-1][...] = out.astype(jnp.bfloat16)

    out = jax.ShapeDtypeStruct((width, columns), jnp.bfloat16)
    return pl.pallas_call(
        kernel,
        grid=(width // block,),
        in_specs=[pl.BlockSpec((total, block), lambda i: (0, i))] * pairs
        + [kept_block((total, columns))] * pairs,
        out_specs=pl.BlockSpec((block, columns), lambda i: (i, 0)),
        out_shape=out,
        compiler_params=kernel_params(),
        cost_estimate=kernel_cost(
            2 * pairs * total * width * columns, out, *rows_of, *columns_of
        ),
    )(*rows_of, *columns_of)


def seg_send(value, counts, step):
    size = lax.axis_size("seg")
    packed = jnp.concatenate([value, counts], axis=1).astype(jnp.bfloat16)
    return [
        lax.ppermute(
            packed,
            "seg",
            [(k, k + step * far) for k in range(size) if 0 <= k + step * far < size],
        )
        for far in range(1, size)
    ]


def seg_sum(arrived):
    total = sum(part.astype(jnp.float32) for part in arrived)
    return (total[:, :-1], total[:, -1:])


def column_half(weight, which):
    half = weight.shape[1] // 2
    return lax.dynamic_slice_in_dim(weight, which * half, half, 1)


def seg_gather(value):
    return lax.all_gather(value, "seg", axis=0, tiled=True)


def other_segments(gathered):
    size, here = (lax.axis_size("seg"), lax.axis_index("seg"))
    rows = gathered.shape[0] // size
    return jnp.concatenate(
        [
            lax.dynamic_slice_in_dim(gathered, lax.rem(here + k, size) * rows, rows, 0)
            for k in range(1, size)
        ],
        axis=0,
    )


def in_order(got, own):
    size, here = (lax.axis_size("seg"), lax.axis_index("seg"))
    turned = jnp.concatenate([got, own], axis=0)
    rows = own.shape[0]
    return jnp.concatenate(
        [
            lax.dynamic_slice_in_dim(turned, lax.rem(size + k - here - 1, size) * rows, rows, 0)
            for k in range(size)
        ],
        axis=0,
    )


def seg_scatter(value):
    return lax.psum_scatter(value, "seg", scatter_dimension=0, tiled=True)


def whole_columns(own, rest):
    first = lax.axis_index("grp") == 0
    return jnp.where(
        first, jnp.concatenate([own, rest], axis=1), jnp.concatenate([rest, own], axis=1)
    ).astype(jnp.float32)


def whole_sum(own, far):
    half = own.shape[1] // 2
    turned = jnp.concatenate([far[:, half:], far[:, :half]], axis=1)
    total = added(own, turned)
    first = lax.axis_index("grp") == 0
    return jnp.where(first, total, jnp.concatenate([total[:, half:], total[:, :half]], axis=1))


def times(left, right):
    return jnp.dot(left, right, preferred_element_type=jnp.float32)


def times_rows(left, right):
    return jnp.einsum("tc,dc->td", left, right, preferred_element_type=jnp.float32)


def weight_grad(rows, columns):
    return jnp.einsum("td,tc->dc", rows, columns, preferred_element_type=jnp.float32)


def root_norm(values, gain):
    return values * lax.rsqrt(jnp.mean(values * values, -1, keepdims=True) + EPS_NORM) * gain


def positive_feature(values):
    return jnp.where(values > 0, values + 1.0, jnp.exp(jnp.where(values > 0, 0.0, values)))


def feature_slope(values):
    return jnp.where(values > 0, 1.0, jnp.exp(jnp.where(values > 0, 0.0, values)))


def dot_as(left, right, dims):
    return lax.dot_general(left, right, (dims, ((), ())), preferred_element_type=jnp.float32)


ROWS_COLUMNS = ((1,), (0,))
BY_COLUMNS = ((1,), (1,))
BY_ROWS = ((0,), (0,))


def head_call(kernel, ins, outs, flops, scratch=()):
    def spec(shape, kind):
        if kind == "smem":
            return pl.BlockSpec(memory_space=pltpu.SMEM)
        if kind == "all":
            return kept_block(shape)
        if kind == "columns":
            return pl.BlockSpec((shape[0], HEAD_DIM), lambda i: (0, i))
        return pl.BlockSpec((1,) + shape[1:], lambda i: (i, 0, 0))

    heads = [s.shape[0] for s, kind in outs if kind == "heads"] + [
        s.shape[1] // HEAD_DIM for s, kind in outs if kind == "columns"
    ]
    return pl.pallas_call(
        kernel,
        grid=(heads[0],),
        in_specs=[spec(a.shape, kind) for a, kind in ins],
        out_specs=[spec(s.shape, kind) for s, kind in outs],
        out_shape=[s for s, kind in outs],
        scratch_shapes=list(scratch),
        compiler_params=kernel_params(),
        cost_estimate=kernel_cost(
            flops, *[a for a, kind in ins if kind != "smem"], *[s for s, kind in outs]
        ),
    )(*[a for a, kind in ins])


def low_feature(values):
    return positive_feature(values.astype(jnp.float32)).astype(jnp.bfloat16)


def like(shape, dtype):
    return jax.ShapeDtypeStruct(shape, dtype)


def features(key_rows, values):
    heads = key_rows.shape[1] // HEAD_DIM

    def kernel(key_ref, value_ref, contrib_ref, count_ref):
        feat_k = low_feature(key_ref[...])
        contrib_ref[0] = dot_as(feat_k, value_ref[...], BY_ROWS)
        count_ref[0] = jnp.sum(feat_k.astype(jnp.float32), axis=0, keepdims=True)

    return head_call(
        kernel,
        [(key_rows, "columns"), (values, "columns")],
        [
            (like((heads, HEAD_DIM, HEAD_DIM), jnp.float32), "heads"),
            (like((heads, 1, HEAD_DIM), jnp.float32), "heads"),
        ],
        2 * SEG_LEN * heads * HEAD_DIM**2,
    )


def reach_of(at):
    return min(SEG_LEN, (at + 2) * PIECE)


def masked_scores(query_block, keys, at, piece_first):
    scores = dot_as(query_block, keys, BY_COLUMNS) * HEAD_DIM ** (-0.5)
    rows_at = at * PIECE + lax.broadcasted_iota(jnp.int32, scores.shape, 0)
    keys_at = lax.broadcasted_iota(jnp.int32, scores.shape, 1)
    row_in = (rows_at >= piece_first) & (rows_at < piece_first + PIECE)
    key_in = (keys_at >= piece_first) & (keys_at < piece_first + PIECE)
    return jnp.where((keys_at <= rows_at) | (row_in & key_in), scores, MASKED_SCORE)


def local_flops(heads, products):
    return products * 2 * heads * HEAD_DIM * PIECE * sum(reach_of(k) for k in range(SEG_LEN // PIECE))


def local_attention(queries, key_rows, values, piece_first):
    heads = queries.shape[1] // HEAD_DIM

    def kernel(first_ref, query_ref, key_ref, value_ref, out_ref, log_ref):
        first = first_ref[0]
        for at in range(SEG_LEN // PIECE):
            rows = slice(at * PIECE, (at + 1) * PIECE)
            reach = reach_of(at)
            scores = masked_scores(query_ref[rows, :], key_ref[:reach, :], at, first)
            peak = jnp.max(scores, axis=-1, keepdims=True)
            shifted = jnp.exp(scores - peak)
            total = jnp.sum(shifted, axis=-1, keepdims=True)
            probs = (shifted * (1.0 / total)).astype(jnp.bfloat16)
            out_ref[rows, :] = dot_as(probs, value_ref[:reach, :], ROWS_COLUMNS)
            log_ref[0, rows, :] = peak + jnp.log(total)

    return head_call(
        kernel,
        [
            (piece_first[None], "smem"),
            (queries, "columns"),
            (key_rows, "columns"),
            (values, "columns"),
        ],
        [
            (like(queries.shape, jnp.float32), "columns"),
            (like((heads, SEG_LEN, 1), jnp.float32), "heads"),
        ],
        local_flops(heads, 2),
    )


def recalled(feat_q, memory, norm_mem):
    numerator = dot_as(feat_q, memory.astype(jnp.bfloat16), ROWS_COLUMNS)
    denominator = 1.0 + jnp.sum(feat_q.astype(jnp.float32) * norm_mem, axis=-1, keepdims=True)
    return (numerator / denominator, denominator)


def mixing(queries, local_out, memory, norm_mem, share):
    heads = queries.shape[1] // HEAD_DIM

    def kernel(share_ref, query_ref, local_ref, memory_ref, norm_ref, out_ref):
        part = share_ref[pl.program_id(0)]
        recall, unused = recalled(low_feature(query_ref[...]), memory_ref[0], norm_ref[0])
        out_ref[...] = (part * recall + (1.0 - part) * local_ref[...]).astype(jnp.bfloat16)

    return head_call(
        kernel,
        [
            (share, "smem"),
            (queries, "columns"),
            (local_out, "columns"),
            (memory, "heads"),
            (norm_mem, "heads"),
        ],
        [(like(queries.shape, jnp.bfloat16), "columns")],
        2 * SEG_LEN * heads * HEAD_DIM**2,
    )[0]


def memory_backward(grad_att, out_full, queries, local_out, memory, norm_mem, share):
    heads = queries.shape[1] // HEAD_DIM

    def kernel(
        share_ref,
        grad_ref,
        weight_ref,
        query_ref,
        local_ref,
        memory_ref,
        norm_ref,
        logit_ref,
        grad_local_ref,
        grad_query_ref,
        grad_memory_ref,
        grad_norm_ref,
    ):
        part = share_ref[pl.program_id(0)]
        queries_f = query_ref[...].astype(jnp.float32)
        feat_q = low_feature(query_ref[...])
        recall, denominator = recalled(feat_q, memory_ref[0], norm_ref[0])
        grad_mixed = dot_as(grad_ref[...], weight_ref[...], ROWS_COLUMNS)
        logit_ref[0] = jnp.sum(grad_mixed * (recall - local_ref[...]), axis=0, keepdims=True)
        grad_local_ref[...] = ((1.0 - part) * grad_mixed).astype(jnp.bfloat16)
        grad_scaled = part * grad_mixed / denominator
        grad_numer = grad_scaled.astype(jnp.bfloat16)
        grad_denom = -jnp.sum(grad_scaled * recall, axis=-1, keepdims=True)
        grad_feat = (
            dot_as(grad_numer, memory_ref[0].astype(jnp.bfloat16), BY_COLUMNS)
            + grad_denom * norm_ref[0]
        )
        grad_query_ref[...] = grad_feat * feature_slope(queries_f)
        grad_memory_ref[0] = dot_as(feat_q, grad_numer, BY_ROWS)
        grad_norm_ref[0] = jnp.sum(feat_q.astype(jnp.float32) * grad_denom, axis=0, keepdims=True)

    square = like((heads, HEAD_DIM, HEAD_DIM), jnp.float32)
    row = like((heads, 1, HEAD_DIM), jnp.float32)
    return head_call(
        kernel,
        [
            (share, "smem"),
            (grad_att, "all"),
            (out_full, "columns"),
            (queries, "columns"),
            (local_out, "columns"),
            (memory, "heads"),
            (norm_mem, "heads"),
        ],
        [
            (row, "heads"),
            (like(queries.shape, jnp.bfloat16), "columns"),
            (like(queries.shape, jnp.float32), "columns"),
            (square, "heads"),
            (row, "heads"),
        ],
        2 * grad_att.size * queries.shape[1] + 6 * SEG_LEN * heads * HEAD_DIM**2,
    )


def local_backward(
    queries, key_rows, values, log_totals, grad_local, grad_query, grad_contrib, grad_count, piece_first
):
    heads = queries.shape[1] // HEAD_DIM

    def kernel(
        first_ref,
        query_ref,
        key_ref,
        value_ref,
        log_ref,
        local_ref,
        memory_ref,
        contrib_ref,
        count_ref,
        query_out,
        key_out,
        value_out,
        key_sum,
        value_sum,
    ):
        first = first_ref[0]
        scale = HEAD_DIM ** (-0.5)
        keys = key_ref[...]
        contrib = contrib_ref[0].astype(jnp.bfloat16)
        grad_feat = dot_as(value_ref[...], contrib, BY_COLUMNS) + count_ref[0]
        key_sum[...] = grad_feat * feature_slope(keys.astype(jnp.float32))
        value_sum[...] = dot_as(low_feature(keys), contrib, ROWS_COLUMNS)
        for at in range(SEG_LEN // PIECE):
            rows = slice(at * PIECE, (at + 1) * PIECE)
            reach = reach_of(at)
            query_block = query_ref[rows, :]
            local_block = local_ref[rows, :]
            scores = masked_scores(query_block, key_ref[:reach, :], at, first)
            probs = jnp.exp(scores - log_ref[0, rows, :])
            grad_probs = dot_as(local_block, value_ref[:reach, :], BY_COLUMNS)
            weighed = probs * grad_probs
            mean = jnp.sum(weighed, axis=-1, keepdims=True)
            grad_scores = (weighed - probs * mean).astype(jnp.bfloat16)
            query_out[rows, :] = (
                dot_as(grad_scores, key_ref[:reach, :], ROWS_COLUMNS) * scale + memory_ref[rows, :]
            ).astype(jnp.bfloat16)
            key_sum[:reach, :] += dot_as(grad_scores, query_block, BY_ROWS) * scale
            value_sum[:reach, :] += dot_as(probs.astype(jnp.bfloat16), local_block, BY_ROWS)
        key_out[...] = key_sum[...].astype(jnp.bfloat16)
        value_out[...] = value_sum[...].astype(jnp.bfloat16)

    out = (like(queries.shape, jnp.bfloat16), "columns")
    return head_call(
        kernel,
        [
            (piece_first[None], "smem"),
            (queries, "columns"),
            (key_rows, "columns"),
            (values, "columns"),
            (log_totals, "heads"),
            (grad_local, "columns"),
            (grad_query, "columns"),
            (grad_contrib, "heads"),
            (grad_count, "heads"),
        ],
        [out, out, out],
        local_flops(heads, 5),
        [pltpu.VMEM((SEG_LEN, HEAD_DIM), jnp.float32)] * 2,
    )


def body(
    hidden_in,
    cotangent,
    piece_start,
    query_weight,
    key_weight,
    value_weight,
    out_weight,
    gate_weight,
    up_weight,
    down_weight,
    attend_gain,
    feed_gain,
    gate_logit,
):
    line = Line(attend_gain)
    group = lax.axis_index("grp")
    count, rows, width = hidden_in.shape
    micros = range(count)
    columns = query_weight.shape[1]
    half = columns // 2
    head_local = columns // HEAD_DIM
    head_turn = group * (head_local // 2)
    heads_here = lax.axis_index("tok") * head_local + lax.rem(
        jnp.arange(head_local, dtype=jnp.int32) + head_turn, head_local
    )
    placement = (
        jnp.arange(HEADS, dtype=jnp.int32)[None, :] == heads_here[:, None]
    ).astype(jnp.float32)
    gate_local = jnp.sum(placement * gate_logit[None, :], axis=1)
    share = jax.nn.sigmoid(gate_local)
    piece_first = [piece_start[m, 0] - lax.axis_index("seg") * SEG_LEN for m in micros]

    def halves(*weights):
        return jnp.concatenate([column_half(w, group) for w in weights], axis=1)

    def other_halves(*weights):
        return jnp.concatenate([column_half(w, 1 - group) for w in weights], axis=1)

    bits = tok_bits()
    here = lax.axis_index("tok")
    order = tok_order(bits)
    spots = jnp.array(order, jnp.int32) ^ here.astype(jnp.int32)
    in_turn = jnp.arange(2 * len(order), dtype=jnp.int32)

    pair_weights = (query_weight, key_weight)
    pair_mine = seg_gather(line(halves, *pair_weights))
    normed_a = line(
        lambda x: root_norm(x.astype(jnp.float32), attend_gain).astype(jnp.bfloat16), hidden_in
    )
    attend_pieces = FirstPiece(normed_a, bits)
    cot_swapped = grp_swap(cotangent)
    value_mine = seg_gather(line(halves, value_weight))
    out_mine = seg_gather(line(halves, out_weight))
    feed_mine = seg_gather(line(halves, gate_weight, up_weight))
    down_mine = seg_gather(line(halves, down_weight))
    pair_other = line(other_halves, *pair_weights)
    value_other = line(other_halves, value_weight)
    out_other = line(other_halves, out_weight)
    cot_swapped = line.hold(cot_swapped)
    attend_pieces = attend_pieces.rest(line)
    cot_pieces = FirstPiece(line.hold(cotangent), bits)
    pair_got = grp_swap(line(other_segments, pair_mine))
    gathered_a = line(
        lambda *p: place(
            p, jnp.concatenate([jnp.stack([s + m * len(order) for m in micros]) for s in spots])
        ),
        *[attend_pieces[at] for at in order],
    )
    gathered_a = [gathered_a[m * SEG_LEN : (m + 1) * SEG_LEN] for m in micros]
    value_got = grp_swap(line(other_segments, value_mine))

    def with_other(mine, got, own, pieces):
        rest = in_order(got, own)
        return tuple(
            jnp.concatenate([part[:, k * half : (k + 1) * half] for part in (mine, rest)], axis=1)
            for k in range(pieces)
        )

    def project(g, *weights):
        return tuple(
            tuple(times(g[m], w).astype(jnp.bfloat16) for m in micros) for w in weights
        )

    query_full, key_full = line(lambda *a: with_other(*a, 2), pair_mine, pair_got, pair_other)
    queries, key_rows = line(project, gathered_a, query_full, key_full)
    cot_pieces = cot_pieces.rest(line)
    cot_far = FirstPiece(cot_swapped, bits)
    (value_full,) = line(lambda *a: with_other(*a, 1), value_mine, value_got, value_other)
    (values,) = line(project, gathered_a, value_full)
    out_got = grp_swap(line(other_segments, out_mine))

    contrib, count_k = zip(*[line(features, key_rows[m], values[m]) for m in micros])
    arrived = seg_send(jnp.concatenate(contrib), jnp.concatenate(count_k), 1)
    local = [
        line(local_attention, queries[m], key_rows[m], values[m], piece_first[m]) for m in micros
    ]
    (out_full,) = line(lambda *a: with_other(*a, 1), out_mine, out_got, out_other)
    cot_far = cot_far.rest(line)
    memory, norm_mem = line(seg_sum, arrived)
    memory = [memory[m * head_local : (m + 1) * head_local] for m in micros]
    norm_mem = [norm_mem[m * head_local : (m + 1) * head_local] for m in micros]
    mixes = []
    attended = []
    for m in micros:
        mixes.append(line(mixing, queries[m], local[m][0], memory[m], norm_mem[m], share))
        attended.append(
            Scatter(*line(lambda a, w: products_cut([a], [w], spots), mixes[m], out_full))
        )
        attended[m].go_on(line)

    def after_attention(x, terms):
        resid = x.astype(jnp.float32) + total_of(terms)
        return (resid, root_norm(resid, feed_gain).astype(jnp.bfloat16))

    resid = []
    feed_pieces = []
    for m in micros:
        rows_m, normed_f = line(after_attention, hidden_in[m], attended[m].terms)
        resid.append(rows_m)
        swapped = grp_swap(normed_f[None])
        feed_pieces.append((tok_pieces(normed_f[None], bits), tok_pieces(swapped, bits)))
        if m == 0:
            feed_mine = line.hold(feed_mine)

    def interleaved(own, far):
        return [pieces[at] for at in order for pieces in (own, far)]

    feed_in = []
    products = []
    inner_act = []
    for m in micros:
        rows_m, both, inner = line(
            lambda w, *p: feed_forward(p, 0, w), feed_mine, *interleaved(*feed_pieces[m])
        )
        feed_in.append(rows_m)
        products.append(both)
        inner_act.append(inner)

    cot_all = []
    grad_products = []
    grad_normed = []

    def backward(m):
        rows_m, grads = line(
            lambda w, both, *p: feed_backward(p, m, w, both),
            down_mine,
            products[m],
            *interleaved(cot_pieces, cot_far),
        )
        cot_all.append(rows_m)
        grad_products.append(grads)

    def backward_rows(m):
        grad_normed.append(
            Scatter(
                *line(
                    lambda a, w: products_cut([a], [w], in_turn), grad_products[m], feed_mine
                )
            )
        )

    def own_and_far(terms):
        total = total_of(terms)
        half = total.shape[0] // 2
        return (total[:half], total[half:].astype(jnp.bfloat16))

    def after_feed_grad(rows_m, own, far, cot):
        unused_norm, pull = jax.vjp(root_norm, rows_m, feed_gain)
        grad_norm, gain_part = pull(added(own, far))
        grad_resid = cot.astype(jnp.float32) + grad_norm
        return (grad_resid, gain_part, grad_resid.astype(jnp.bfloat16))

    grad_parts = []
    grad_resid = []
    feed_gain_parts = []
    att_pieces = []

    def finish_rows(m):
        own, far = line(own_and_far, grad_normed[m].terms)
        grad_parts.append((own, grp_swap(far)))

    def finish_feed(m):
        rows_m, gain_part, low = line(after_feed_grad, resid[m], *grad_parts[m], cotangent[m])
        grad_resid.append(rows_m)
        feed_gain_parts.append(gain_part)
        att_pieces.append(tok_pieces(low[None], bits))

    feed_out = []

    def feed_result(m):
        feed_out.append(
            Scatter(
                *line(lambda a, w: products_cut([a], [w], in_turn), inner_act[m], down_mine)
            )
        )

    backward(0)
    backward_rows(0)
    backward(1)
    down_grad = seg_scatter(line(grad_product, cot_all, inner_act))
    grad_normed[0].go_on(line)
    backward_rows(1)
    feed_grad = seg_scatter(line(grad_product, feed_in, grad_products))
    grad_normed[1].go_on(line)
    finish_rows(0)
    feed_result(0)
    finish_rows(1)
    finish_feed(0)
    feed_result(1)
    finish_feed(1)

    grad_att = []
    mem_back = []
    for m in micros:
        grad_att.append(
            line(lambda *p: place(p, spots), *[att_pieces[m][at] for at in order])
        )
        mem_back.append(
            line(
                memory_backward,
                grad_att[m],
                out_full,
                queries[m],
                local[m][0],
                memory[m],
                norm_mem[m],
                share,
            )
        )
    logit_parts, grad_local, grad_query, grad_memory, grad_norm_mem = zip(*mem_back)
    back_arrived = seg_send(jnp.concatenate(grad_memory), jnp.concatenate(grad_norm_mem), -1)
    for m in micros:
        feed_out[m].go_on(line)
    down_grad = line.hold(down_grad)
    down_rest = grp_swap(down_grad)

    def half_grad(which, rows_of, *columns_of):
        return sum(
            weight_grad(
                a,
                jnp.concatenate(
                    [
                        c[m] if which is None else c[m][:, which * half : (which + 1) * half]
                        for c in columns_of
                    ],
                    axis=1,
                ),
            )
            for m, a in enumerate(rows_of)
        )

    mixed_rows = mixes
    out_far = grp_swap(
        line(lambda a, b: half_grad(1, a, b).astype(jnp.bfloat16), grad_att, mixed_rows)
    )
    out_grad = seg_scatter(
        line(
            lambda a, b, far: (half_grad(0, a, b) + far.astype(jnp.float32)).astype(jnp.bfloat16),
            grad_att,
            mixed_rows,
            out_far,
        )
    )
    feed_parts = []
    for m in micros:
        own, far = line(own_and_far, feed_out[m].terms)
        feed_parts.append((own, grp_swap(far)))
    grad_contrib, grad_count = line(seg_sum, back_arrived)
    feed_grad = line.hold(feed_grad)
    feed_rest = grp_swap(feed_grad)
    low_grads = []
    for m in micros:
        low_grads.append(
            line(
                local_backward,
                queries[m],
                key_rows[m],
                values[m],
                local[m][1],
                grad_local[m],
                grad_query[m],
                grad_contrib[m * head_local : (m + 1) * head_local],
                grad_count[m * head_local : (m + 1) * head_local],
                piece_first[m],
            )
        )
    query_low, key_low, value_low = zip(*low_grads)
    gathered_list = gathered_a
    query_sum = seg_scatter(
        line(lambda a, b: half_grad(None, a, b).astype(jnp.bfloat16), gathered_list, query_low)
    )
    pair_far = grp_swap(
        line(
            lambda *a: half_grad(1, *a).astype(jnp.bfloat16), gathered_list, key_low, value_low
        )
    )
    grad_normed_a = []
    for m in micros:
        grad_normed_a.append(
            Scatter(
                *line(
                    lambda a, b, c, wa, wb, wc: products_cut([a, b, c], [wa, wb, wc], spots),
                    query_low[m],
                    key_low[m],
                    value_low[m],
                    query_full,
                    key_full,
                    value_full,
                )
            )
        )
    for m in micros:
        grad_normed_a[m].go_on(line)
    out_grad = line.hold(out_grad)
    out_rest = grp_swap(out_grad)
    pair_grad = seg_scatter(
        line(
            lambda far, *a: (half_grad(0, *a) + far.astype(jnp.float32)).astype(jnp.bfloat16),
            pair_far,
            gathered_list,
            key_low,
            value_low,
        )
    )

    def after_attend_grad(x, terms, grad, gain):
        unused_norm, pull = jax.vjp(root_norm, x.astype(jnp.float32), gain)
        grad_norm, gain_part = pull(total_of(terms))
        return ((grad + grad_norm).astype(jnp.bfloat16), gain_part)

    input_rows = []
    attend_gain_parts = []
    for m in micros:
        grad_rows, gain_part = line(
            after_attend_grad, hidden_in[m], grad_normed_a[m].terms, grad_resid[m], line.token
        )
        input_rows.append(grad_rows)
        attend_gain_parts.append(gain_part)
    gate_logit_part = jnp.sum(sum(logit_parts), axis=(1, 2)) * share * (1.0 - share)
    gate_full_grad = jnp.sum(placement * gate_logit_part[:, None], axis=0)
    small = line(
        lambda a, b, c: jnp.concatenate([sum(a), sum(b), c])[None],
        attend_gain_parts,
        feed_gain_parts,
        gate_full_grad,
    )
    out_out = line(whole_columns, out_grad, out_rest)
    down_out = line(whole_columns, down_grad, down_rest)
    feed_half = gate_weight.shape[1] // 2
    gate_out, up_out = line(
        lambda a, b: tuple(
            whole_columns(*[part[:, k * feed_half : (k + 1) * feed_half] for part in (a, b)])
            for k in range(2)
        ),
        feed_grad,
        feed_rest,
    )
    query_sum = line.hold(query_sum)
    query_rest = grp_swap(query_sum)
    for axis in ("tok", "seg", "grp"):
        size = lax.axis_size(axis)
        for bit in [1 << k for k in range(size.bit_length() - 1)]:
            other = lax.ppermute(small, axis, [(k, k ^ bit) for k in range(size)])
            small = line(jnp.add, small, other)
    output_rows = [
        line(
            lambda r, own, far: (r + added(own, far)).astype(jnp.bfloat16), resid[m], *feed_parts[m]
        )
        for m in micros
    ]
    query_grad = line(whole_sum, query_sum, query_rest)
    pair_rest = grp_swap(pair_grad)
    key_grad, value_grad = line(
        lambda a, b: tuple(
            whole_columns(*[part[:, k * half : (k + 1) * half] for part in (a, b)])
            for k in range(2)
        ),
        pair_grad,
        pair_rest,
    )
    small_sums = (small[0, :width], small[0, width : 2 * width], small[0, 2 * width :])
    return (
        (jnp.stack(output_rows), jnp.stack(input_rows))
        + (query_grad, key_grad, value_grad)
        + (out_out, gate_out, up_out, down_out)
        + small_sums
    )


def solution(mesh):
    return jax.shard_map(
        body,
        mesh=mesh,
        in_specs=(
            P("grp", ("seg", "tok"), None),
            P("grp", ("seg", "tok"), None),
            P("grp", "seg"),
            P("seg", "tok"),
            P("seg", "tok"),
            P("seg", "tok"),
            P("seg", "tok"),
            P("seg", "tok"),
            P("seg", "tok"),
            P("seg", "tok"),
            P(),
            P(),
            P(),
        ),
        out_specs=(
            P("grp", ("seg", "tok"), None),
            P("grp", ("seg", "tok"), None),
            P("seg", "tok"),
            P("seg", "tok"),
            P("seg", "tok"),
            P("seg", "tok"),
            P("seg", "tok"),
            P("seg", "tok"),
            P("seg", "tok"),
            P(),
            P(),
            P(),
        ),
        check_vma=False,
    )
```

```python
import jax
import jax.numpy as jnp
from jax import lax
from jax.experimental import pallas as pl
from jax.experimental.pallas import tpu as pltpu
from jax.sharding import PartitionSpec as P

HEADS = 16
HEAD_DIM = 128
SEG_LEN = 1024
PIECE = 256
VMEM_BYTES = 60 * 1024 * 1024
MICRO = 2


EPS_NORM = 1e-05
MASKED_SCORE = -1e30


class Line:
    def __init__(self, token):
        self.token = token

    def hold(self, value):
        value, self.token = lax.optimization_barrier((value, self.token))
        return value

    def __call__(self, step, *inputs):
        return self.hold(step(*self.hold(inputs)))


def tok_bits():
    return [1 << k for k in range(lax.axis_size("tok").bit_length() - 1)]


def tok_swap(value, bit):
    count = lax.axis_size("tok")
    return lax.ppermute(value, "tok", [(k, k ^ bit) for k in range(count)])


def tok_at(bit):
    return jnp.where((lax.axis_index("tok") & bit) == 0, 0, 1)


def grp_swap(value):
    return lax.ppermute(value, "grp", [(0, 1), (1, 0)])


def tok_pieces(rows, bits):
    pieces = {0: rows}
    for bit in reversed(bits):
        for at in sorted(pieces):
            pieces[at | bit] = tok_swap(pieces[at], bit)
    return pieces


def joined(near, far, bit):
    return {**near, **{at | bit: piece for at, piece in far.items()}}


class BothGroups:
    def __init__(self, rows, bits, over_tok=None):
        self.low, self.high = (bits[:-1], bits[-1])
        self.tok_first = over_tok is not None
        self.rows = rows
        self.swapped = tok_swap(over_tok if self.tok_first else rows, self.high)
        self.got = grp_swap(rows)

    def go_on(self, line):
        if self.tok_first:
            self.swapped = line.hold(self.swapped)
            self.late = grp_swap(self.swapped)
        else:
            self.late = tok_swap(self.got, self.high)
        self.own = joined(
            tok_pieces(self.rows, self.low), tok_pieces(self.swapped, self.low), self.high
        )
        self.far = tok_pieces(self.got, self.low)

    def finish(self, line):
        late = tok_pieces(line.hold(self.late), self.low)
        return (self.own, joined(self.far, late, self.high))


class FirstPiece:
    def __init__(self, rows, bits):
        self.rows = rows
        self.bits = bits
        self.got = tok_swap(rows, bits[-1])

    def rest(self, line):
        pieces = {0: self.rows, self.bits[-1]: line.hold(self.got)}
        for bit in reversed(self.bits[:-1]):
            for at in sorted(pieces):
                pieces[at | bit] = tok_swap(pieces[at], bit)
        return pieces


def added(kept, got):
    return kept.astype(jnp.float32) + got.astype(jnp.float32)


class Scatter:
    def __init__(self, kept, sent):
        self.bits = tok_bits()
        self.terms = (kept, tok_swap(sent, self.bits[0]))

    def go_on(self, line):
        def cut(*terms):
            rows = terms[-1].shape[0]
            return sum(term[rows // 2 : rows].astype(jnp.float32) for term in terms).astype(
                jnp.bfloat16
            )

        for bit in self.bits[1:]:
            self.terms = self.terms + (tok_swap(line(cut, *self.terms), bit),)


def total_of(terms):
    rows = terms[-1].shape[0]
    return sum(term[:rows].astype(jnp.float32) for term in terms)


def tok_order(bits):
    order = [0]
    for bit in reversed(bits):
        order = order + [at | bit for at in order]
    return order


def kernel_params():
    return pltpu.CompilerParams(vmem_limit_bytes=VMEM_BYTES)


def kernel_cost(flops, *arrays):
    moved = sum(a.size * a.dtype.itemsize for a in arrays)
    return pl.CostEstimate(flops=flops, transcendentals=0, bytes_accessed=moved)


def any_space():
    return pl.BlockSpec(memory_space=pl.ANY)


def kept_block(shape):
    return pl.BlockSpec(shape, lambda *at: (0,) * len(shape), pipeline_mode=pl.Buffered(1))


def place(pieces, order, here):
    rows, width = pieces[0].shape[-2:]
    total = sum(p.shape[0] for p in pieces)

    def kernel(here_ref, *refs):
        *ins, out, held, arrive, leave = refs
        copies = []
        for mask, ref in zip(order, ins):
            for j in range(ref.shape[0]):
                at = len(copies)
                spot = j * len(order) + (here_ref[0] ^ mask)
                start = pl.multiple_of(spot * rows, rows)
                copies.append(
                    (
                        pltpu.make_async_copy(ref.at[j], held.at[at], arrive.at[at]),
                        pltpu.make_async_copy(
                            held.at[at], out.at[pl.ds(start, rows)], leave.at[at]
                        ),
                    )
                )
        for first, _ in copies:
            first.start()
        for first, then in copies:
            first.wait()
            then.start()
        for _, then in copies:
            then.wait()

    out = jax.ShapeDtypeStruct((total * rows, width), pieces[0].dtype)
    return pl.pallas_call(
        kernel,
        in_specs=[pl.BlockSpec(memory_space=pltpu.SMEM)] + [any_space()] * len(pieces),
        out_specs=any_space(),
        out_shape=out,
        scratch_shapes=[
            pltpu.VMEM((total, rows, width), pieces[0].dtype),
            pltpu.SemaphoreType.DMA((total,)),
            pltpu.SemaphoreType.DMA((total,)),
        ],
        compiler_params=kernel_params(),
        cost_estimate=kernel_cost(0, out, out),
    )(here, *pieces)


def over_pieces(pieces, which, extra, extra_specs, outs, compute, flops):
    rows, width = pieces[0].shape[-2:]
    total = rows * len(pieces)
    block = max(rows, min(512, total))
    each = block // rows

    def kernel(*refs):
        ins = refs[: len(pieces)]
        others = refs[len(pieces) : len(pieces) + len(extra)]
        results = refs[len(pieces) + len(extra) : -2]
        held, arrive = refs[-2:]
        step = pl.program_id(0)

        def copy(at, ref):
            return pltpu.make_async_copy(
                ref.at[which], held.at[pl.ds(at * rows, rows)], arrive.at[at]
            )

        @pl.when(step == 0)
        def start_all():
            for at, ref in enumerate(ins):
                copy(at, ref).start()

        for part in range(each):
            copy(step * each + part, ins[0]).wait()
        x = held[pl.ds(pl.multiple_of(step * block, block), block)]
        results[0][...] = x
        compute(x, others, results[1:])

    row_spec = lambda n: pl.BlockSpec((block, n), lambda i: (i, 0))
    shapes = [jax.ShapeDtypeStruct((total, n), jnp.bfloat16) for n in (width,) + tuple(outs)]
    return pl.pallas_call(
        kernel,
        grid=(total // block,),
        in_specs=[any_space()] * len(pieces) + [spec(row_spec) for spec in extra_specs],
        out_specs=[row_spec(s.shape[1]) for s in shapes],
        out_shape=shapes,
        scratch_shapes=[
            pltpu.VMEM((total, width), pieces[0].dtype),
            pltpu.SemaphoreType.DMA((len(pieces),)),
        ],
        compiler_params=kernel_params(),
        cost_estimate=kernel_cost(flops, *shapes, *extra),
    )(*pieces, *extra)


def feed_forward(pieces, which, weight):
    hidden = weight.shape[1] // 2
    total = len(pieces) * pieces[0].shape[-2]

    def compute(x, others, results):
        both = jnp.dot(x, others[0][...], preferred_element_type=jnp.float32)
        gate, up = (both[:, :hidden], both[:, hidden:])
        results[0][...] = both.astype(jnp.bfloat16)
        results[1][...] = (gate * jax.nn.sigmoid(gate) * up).astype(jnp.bfloat16)

    return over_pieces(
        pieces,
        which,
        (weight,),
        (lambda row_spec: kept_block(weight.shape),),
        (2 * hidden, hidden),
        compute,
        2 * total * weight.size,
    )


def feed_backward(pieces, which, weight, both):
    hidden = weight.shape[1]
    total = len(pieces) * pieces[0].shape[-2]

    def compute(x, others, results):
        grad = jnp.dot(x, others[0][...], preferred_element_type=jnp.float32)
        gate = others[1][:, :hidden].astype(jnp.float32)
        up = others[1][:, hidden:].astype(jnp.float32)
        sig = jax.nn.sigmoid(gate)
        results[0][:, :hidden] = (grad * up * sig * (1.0 + gate * (1.0 - sig))).astype(jnp.bfloat16)
        results[0][:, hidden:] = (grad * gate * sig).astype(jnp.bfloat16)

    return over_pieces(
        pieces,
        which,
        (weight, both),
        (lambda row_spec: kept_block(weight.shape), lambda row_spec: row_spec(2 * hidden)),
        (2 * hidden,),
        compute,
        2 * total * weight.size,
    )


def products_cut(lefts, weights, order):
    total, width = (lefts[0].shape[0], weights[0].shape[0])
    steps = order.shape[0]
    rows = total // steps
    half = steps // 2
    pairs = len(lefts)

    def kernel(order_ref, *refs):
        out = 0.0
        for left, weight in zip(refs[:pairs], refs[pairs : 2 * pairs]):
            out = out + lax.dot_general(
                left[...],
                weight[...],
                (((1,), (1,)), ((), ())),
                preferred_element_type=jnp.float32,
            )
        sent_ref, kept_ref = refs[2 * pairs :]
        step = pl.program_id(0)

        @pl.when(step < half)
        def first_part():
            sent_ref[...] = out.astype(jnp.bfloat16)

        @pl.when(step >= half)
        def second_part():
            kept_ref[...] = out.astype(jnp.bfloat16)

    part = jax.ShapeDtypeStruct((total // 2, width), jnp.bfloat16)
    sent, kept = pl.pallas_call(
        kernel,
        grid_spec=pltpu.PrefetchScalarGridSpec(
            num_scalar_prefetch=1,
            grid=(steps,),
            in_specs=[
                pl.BlockSpec(
                    (rows, left.shape[1]), lambda i, at: (at[lax.rem(i + half, steps)], 0)
                )
                for left in lefts
            ]
            + [kept_block(weight.shape) for weight in weights],
            out_specs=[
                pl.BlockSpec((rows, width), lambda i, at: (jnp.minimum(i, half - 1), 0)),
                pl.BlockSpec((rows, width), lambda i, at: (jnp.maximum(i - half, 0), 0)),
            ],
        ),
        out_shape=[part, part],
        compiler_params=kernel_params(),
        cost_estimate=kernel_cost(
            sum(2 * total * weight.size for weight in weights), part, part, *lefts, *weights
        ),
    )(order, *lefts, *weights)
    return (kept, sent)


def grad_product(rows_of, columns_of, which=None, far=None):
    sets = len(columns_of)
    count = len(rows_of)
    total, width = rows_of[0].shape
    columns = columns_of[0][0].shape[1]
    part, at = (columns, 0) if which is None else (columns // 2, which)
    block = 256
    narrow = part % 128 != 0

    def kernel(*refs):
        rows = refs[:count]
        for k in range(sets):
            out = 0.0
            for left, right in zip(rows, refs[count + k * count : count + (k + 1) * count]):
                right = right[:, at * part : (at + 1) * part] if narrow else right[...]
                out = out + lax.dot_general(
                    left[...],
                    right,
                    (((0,), (0,)), ((), ())),
                    preferred_element_type=jnp.float32,
                )
            cut = slice(k * part, (k + 1) * part)
            if far is not None:
                out = out + refs[-2][:, cut].astype(jnp.float32)
            refs[-1][:, cut] = out.astype(jnp.bfloat16)

    out = jax.ShapeDtypeStruct((width, sets * part), jnp.bfloat16)
    flat_columns = [c for columns_set in columns_of for c in columns_set]
    column_spec = pl.BlockSpec(
        (total, columns) if narrow else (total, part),
        lambda i: (0, 0 if narrow else at),
        pipeline_mode=pl.Buffered(1),
    )
    out_spec = pl.BlockSpec((block, sets * part), lambda i: (i, 0))
    extra = [] if far is None else [far]
    return pl.pallas_call(
        kernel,
        grid=(width // block,),
        in_specs=[pl.BlockSpec((total, block), lambda i: (0, i))] * count
        + [column_spec] * len(flat_columns)
        + [out_spec] * len(extra),
        out_specs=out_spec,
        out_shape=out,
        compiler_params=kernel_params(),
        cost_estimate=kernel_cost(
            2 * count * total * width * part * sets, out, *rows_of, *flat_columns
        ),
    )(*rows_of, *flat_columns, *extra)


def seg_send(value, counts, step):
    size = lax.axis_size("seg")
    packed = jnp.concatenate([value, counts], axis=1).astype(jnp.bfloat16)
    return [
        lax.ppermute(
            packed,
            "seg",
            [(k, k + step * far) for k in range(size) if 0 <= k + step * far < size],
        )
        for far in range(1, size)
    ]


def seg_sum(arrived):
    total = sum(part.astype(jnp.float32) for part in arrived)
    return (total[:, :-1], total[:, -1:])


def column_half(weight, which):
    half = weight.shape[1] // 2
    return lax.dynamic_slice_in_dim(weight, which * half, half, 1)


def seg_gather(value):
    return lax.all_gather(value, "seg", axis=0, tiled=True)


def other_segments(gathered):
    size, here = (lax.axis_size("seg"), lax.axis_index("seg"))
    rows = gathered.shape[0] // size
    return jnp.concatenate(
        [
            lax.dynamic_slice_in_dim(gathered, lax.rem(here + k, size) * rows, rows, 0)
            for k in range(1, size)
        ],
        axis=0,
    )


def with_other(mine, got, own, pieces):
    size = mine.shape[0] // own.shape[0]
    rows, half = (own.shape[0], own.shape[1] // pieces)
    here = lax.axis_index("seg").astype(jnp.int32)[None]

    def kernel(here_ref, mine_ref, got_ref, own_ref, *outs):
        is_own = pl.program_id(0) == here_ref[0]
        rest = jnp.where(is_own, own_ref[...], got_ref[...])
        for k, out in enumerate(outs):
            cut = slice(k * half, (k + 1) * half)
            out[:, :half] = mine_ref[:, cut]
            out[:, half:] = rest[:, cut]

    def got_block(i, at):
        return (jnp.minimum(lax.rem(i + size - at[0] - 1 + size, size), size - 2), 0)

    out = jax.ShapeDtypeStruct((mine.shape[0], 2 * half), mine.dtype)
    return pl.pallas_call(
        kernel,
        grid_spec=pltpu.PrefetchScalarGridSpec(
            num_scalar_prefetch=1,
            grid=(size,),
            in_specs=[
                pl.BlockSpec((rows, own.shape[1]), lambda i, at: (i, 0)),
                pl.BlockSpec((rows, own.shape[1]), got_block),
                pl.BlockSpec((rows, own.shape[1]), lambda i, at: (0, 0)),
            ],
            out_specs=[pl.BlockSpec((rows, 2 * half), lambda i, at: (i, 0))] * pieces,
        ),
        out_shape=[out] * pieces,
        compiler_params=kernel_params(),
        cost_estimate=kernel_cost(0, mine, mine, mine, mine),
    )(here, mine, got, own)


def seg_scatter(value):
    return lax.psum_scatter(value, "seg", scatter_dimension=0, tiled=True)


def whole_columns(own, rest):
    first = lax.axis_index("grp") == 0
    return jnp.where(
        first, jnp.concatenate([own, rest], axis=1), jnp.concatenate([rest, own], axis=1)
    ).astype(jnp.float32)


def whole_sum(own, far):
    half = own.shape[1] // 2
    turned = jnp.concatenate([far[:, half:], far[:, :half]], axis=1)
    total = added(own, turned)
    first = lax.axis_index("grp") == 0
    return jnp.where(first, total, jnp.concatenate([total[:, half:], total[:, :half]], axis=1))


def times(left, right):
    return jnp.dot(left, right, preferred_element_type=jnp.float32)


def times_rows(left, right):
    return jnp.einsum("tc,dc->td", left, right, preferred_element_type=jnp.float32)


def weight_grad(rows, columns):
    return jnp.einsum("td,tc->dc", rows, columns, preferred_element_type=jnp.float32)


def root_norm(values, gain):
    return values * lax.rsqrt(jnp.mean(values * values, -1, keepdims=True) + EPS_NORM) * gain


def positive_feature(values):
    return jnp.where(values > 0, values + 1.0, jnp.exp(jnp.where(values > 0, 0.0, values)))


def feature_slope(values):
    return jnp.where(values > 0, 1.0, jnp.exp(jnp.where(values > 0, 0.0, values)))


def dot_as(left, right, dims):
    return lax.dot_general(left, right, (dims, ((), ())), preferred_element_type=jnp.float32)


ROWS_COLUMNS = ((1,), (0,))
BY_COLUMNS = ((1,), (1,))
BY_ROWS = ((0,), (0,))


def head_call(kernel, ins, outs, flops, scratch=()):
    def spec(shape, kind):
        if kind == "smem":
            return pl.BlockSpec(memory_space=pltpu.SMEM)
        if kind == "all":
            return kept_block(shape)
        if kind == "columns":
            return pl.BlockSpec((shape[0], HEAD_DIM), lambda i: (0, i))
        return pl.BlockSpec((1,) + shape[1:], lambda i: (i, 0, 0))

    heads = [s.shape[0] for s, kind in outs if kind == "heads"] + [
        s.shape[1] // HEAD_DIM for s, kind in outs if kind == "columns"
    ]
    return pl.pallas_call(
        kernel,
        grid=(heads[0],),
        in_specs=[spec(a.shape, kind) for a, kind in ins],
        out_specs=[spec(s.shape, kind) for s, kind in outs],
        out_shape=[s for s, kind in outs],
        scratch_shapes=list(scratch),
        compiler_params=kernel_params(),
        cost_estimate=kernel_cost(
            flops, *[a for a, kind in ins if kind != "smem"], *[s for s, kind in outs]
        ),
    )(*[a for a, kind in ins])


def low_feature(values):
    return positive_feature(values.astype(jnp.float32)).astype(jnp.bfloat16)


def like(shape, dtype):
    return jax.ShapeDtypeStruct(shape, dtype)


def features(key_rows, values):
    heads = key_rows.shape[1] // HEAD_DIM

    def kernel(key_ref, value_ref, contrib_ref, count_ref):
        feat_k = low_feature(key_ref[...])
        contrib_ref[0] = dot_as(feat_k, value_ref[...], BY_ROWS)
        count_ref[0] = jnp.sum(feat_k.astype(jnp.float32), axis=0, keepdims=True)

    return head_call(
        kernel,
        [(key_rows, "columns"), (values, "columns")],
        [
            (like((heads, HEAD_DIM, HEAD_DIM), jnp.float32), "heads"),
            (like((heads, 1, HEAD_DIM), jnp.float32), "heads"),
        ],
        2 * SEG_LEN * heads * HEAD_DIM**2,
    )


def reach_of(at):
    return min(SEG_LEN, (at + 2) * PIECE)


def masked_scores(query_block, keys, at, piece_first):
    scores = dot_as(query_block, keys, BY_COLUMNS) * HEAD_DIM ** (-0.5)
    rows_at = at * PIECE + lax.broadcasted_iota(jnp.int32, scores.shape, 0)
    keys_at = lax.broadcasted_iota(jnp.int32, scores.shape, 1)
    row_in = (rows_at >= piece_first) & (rows_at < piece_first + PIECE)
    key_in = (keys_at >= piece_first) & (keys_at < piece_first + PIECE)
    return jnp.where((keys_at <= rows_at) | (row_in & key_in), scores, MASKED_SCORE)


def local_flops(heads, products):
    return products * 2 * heads * HEAD_DIM * PIECE * sum(reach_of(k) for k in range(SEG_LEN // PIECE))


def local_attention(queries, key_rows, values, piece_first):
    heads = queries.shape[1] // HEAD_DIM

    def kernel(first_ref, query_ref, key_ref, value_ref, out_ref, log_ref):
        first = first_ref[0]
        for at in range(SEG_LEN // PIECE):
            rows = slice(at * PIECE, (at + 1) * PIECE)
            reach = reach_of(at)
            scores = masked_scores(query_ref[rows, :], key_ref[:reach, :], at, first)
            peak = jnp.max(scores, axis=-1, keepdims=True)
            shifted = jnp.exp(scores - peak)
            total = jnp.sum(shifted, axis=-1, keepdims=True)
            probs = (shifted * (1.0 / total)).astype(jnp.bfloat16)
            out_ref[rows, :] = dot_as(probs, value_ref[:reach, :], ROWS_COLUMNS)
            log_ref[0, rows, :] = peak + jnp.log(total)

    return head_call(
        kernel,
        [
            (piece_first[None], "smem"),
            (queries, "columns"),
            (key_rows, "columns"),
            (values, "columns"),
        ],
        [
            (like(queries.shape, jnp.float32), "columns"),
            (like((heads, SEG_LEN, 1), jnp.float32), "heads"),
        ],
        local_flops(heads, 2),
    )


def recalled(feat_q, memory, norm_mem):
    numerator = dot_as(feat_q, memory.astype(jnp.bfloat16), ROWS_COLUMNS)
    denominator = 1.0 + jnp.sum(feat_q.astype(jnp.float32) * norm_mem, axis=-1, keepdims=True)
    return (numerator / denominator, denominator)


def mixing(queries, local_out, memory, norm_mem, share):
    heads = queries.shape[1] // HEAD_DIM

    def kernel(share_ref, query_ref, local_ref, memory_ref, norm_ref, out_ref):
        part = share_ref[pl.program_id(0)]
        recall, unused = recalled(low_feature(query_ref[...]), memory_ref[0], norm_ref[0])
        out_ref[...] = (part * recall + (1.0 - part) * local_ref[...]).astype(jnp.bfloat16)

    return head_call(
        kernel,
        [
            (share, "smem"),
            (queries, "columns"),
            (local_out, "columns"),
            (memory, "heads"),
            (norm_mem, "heads"),
        ],
        [(like(queries.shape, jnp.bfloat16), "columns")],
        2 * SEG_LEN * heads * HEAD_DIM**2,
    )[0]


def memory_backward(grad_att, out_full, queries, local_out, memory, norm_mem, share):
    heads = queries.shape[1] // HEAD_DIM

    def kernel(
        share_ref,
        grad_ref,
        weight_ref,
        query_ref,
        local_ref,
        memory_ref,
        norm_ref,
        logit_ref,
        grad_local_ref,
        grad_query_ref,
        grad_memory_ref,
        grad_norm_ref,
    ):
        part = share_ref[pl.program_id(0)]
        queries_f = query_ref[...].astype(jnp.float32)
        feat_q = low_feature(query_ref[...])
        recall, denominator = recalled(feat_q, memory_ref[0], norm_ref[0])
        grad_mixed = dot_as(grad_ref[...], weight_ref[...], ROWS_COLUMNS)
        logit_ref[0] = jnp.sum(grad_mixed * (recall - local_ref[...]), axis=0, keepdims=True)
        grad_local_ref[...] = ((1.0 - part) * grad_mixed).astype(jnp.bfloat16)
        grad_scaled = part * grad_mixed / denominator
        grad_numer = grad_scaled.astype(jnp.bfloat16)
        grad_denom = -jnp.sum(grad_scaled * recall, axis=-1, keepdims=True)
        grad_feat = (
            dot_as(grad_numer, memory_ref[0].astype(jnp.bfloat16), BY_COLUMNS)
            + grad_denom * norm_ref[0]
        )
        grad_query_ref[...] = grad_feat * feature_slope(queries_f)
        grad_memory_ref[0] = dot_as(feat_q, grad_numer, BY_ROWS)
        grad_norm_ref[0] = jnp.sum(feat_q.astype(jnp.float32) * grad_denom, axis=0, keepdims=True)

    square = like((heads, HEAD_DIM, HEAD_DIM), jnp.float32)
    row = like((heads, 1, HEAD_DIM), jnp.float32)
    return head_call(
        kernel,
        [
            (share, "smem"),
            (grad_att, "all"),
            (out_full, "columns"),
            (queries, "columns"),
            (local_out, "columns"),
            (memory, "heads"),
            (norm_mem, "heads"),
        ],
        [
            (row, "heads"),
            (like(queries.shape, jnp.bfloat16), "columns"),
            (like(queries.shape, jnp.float32), "columns"),
            (square, "heads"),
            (row, "heads"),
        ],
        2 * grad_att.size * queries.shape[1] + 6 * SEG_LEN * heads * HEAD_DIM**2,
    )


def local_backward(queries, key_rows, values, log_totals, grad_local, grad_query, piece_first):
    heads = queries.shape[1] // HEAD_DIM

    def kernel(
        first_ref,
        query_ref,
        key_ref,
        value_ref,
        log_ref,
        local_ref,
        memory_ref,
        query_out,
        key_out,
        value_out,
    ):
        first = first_ref[0]
        scale = HEAD_DIM ** (-0.5)
        for at in range(SEG_LEN // PIECE):
            rows = slice(at * PIECE, (at + 1) * PIECE)
            reach = reach_of(at)
            known = reach_of(at - 1) if at > 0 else 0
            query_block = query_ref[rows, :]
            local_block = local_ref[rows, :]
            scores = masked_scores(query_block, key_ref[:reach, :], at, first)
            probs = jnp.exp(scores - log_ref[0, rows, :])
            grad_probs = dot_as(local_block, value_ref[:reach, :], BY_COLUMNS)
            weighed = probs * grad_probs
            mean = jnp.sum(weighed, axis=-1, keepdims=True)
            grad_scores = (weighed - probs * mean).astype(jnp.bfloat16)
            query_out[rows, :] = (
                dot_as(grad_scores, key_ref[:reach, :], ROWS_COLUMNS) * scale + memory_ref[rows, :]
            ).astype(jnp.bfloat16)
            for out, part in (
                (key_out, dot_as(grad_scores, query_block, BY_ROWS) * scale),
                (value_out, dot_as(probs.astype(jnp.bfloat16), local_block, BY_ROWS)),
            ):
                if known > 0:
                    out[:known, :] += part[:known]
                if known < reach:
                    out[known:reach, :] = part[known:]

    wide = (like(queries.shape, jnp.float32), "columns")
    return head_call(
        kernel,
        [
            (piece_first[None], "smem"),
            (queries, "columns"),
            (key_rows, "columns"),
            (values, "columns"),
            (log_totals, "heads"),
            (grad_local, "columns"),
            (grad_query, "columns"),
        ],
        [(like(queries.shape, jnp.bfloat16), "columns"), wide, wide],
        local_flops(heads, 5),
    )


def with_memory(key_rows, values, key_sum, value_sum, grad_contrib, grad_count):
    heads = key_rows.shape[1] // HEAD_DIM

    def kernel(key_ref, value_ref, key_sum, value_sum, contrib_ref, count_ref, key_out, value_out):
        keys = key_ref[...]
        contrib = contrib_ref[0].astype(jnp.bfloat16)
        grad_feat = dot_as(value_ref[...], contrib, BY_COLUMNS) + count_ref[0]
        slope = feature_slope(keys.astype(jnp.float32))
        key_out[...] = (key_sum[...] + grad_feat * slope).astype(jnp.bfloat16)
        value_out[...] = (
            value_sum[...] + dot_as(low_feature(keys), contrib, ROWS_COLUMNS)
        ).astype(jnp.bfloat16)

    out = (like(key_rows.shape, jnp.bfloat16), "columns")
    return head_call(
        kernel,
        [
            (key_rows, "columns"),
            (values, "columns"),
            (key_sum, "columns"),
            (value_sum, "columns"),
            (grad_contrib, "heads"),
            (grad_count, "heads"),
        ],
        [out, out],
        4 * SEG_LEN * heads * HEAD_DIM**2,
    )


def body(
    hidden_in,
    cotangent,
    piece_start,
    query_weight,
    key_weight,
    value_weight,
    out_weight,
    gate_weight,
    up_weight,
    down_weight,
    attend_gain,
    feed_gain,
    gate_logit,
):
    line = Line(attend_gain)
    group = lax.axis_index("grp")
    count, rows, width = hidden_in.shape
    micros = range(count)
    columns = query_weight.shape[1]
    half = columns // 2
    head_local = columns // HEAD_DIM
    head_turn = group * (head_local // 2)
    heads_here = lax.axis_index("tok") * head_local + lax.rem(
        jnp.arange(head_local, dtype=jnp.int32) + head_turn, head_local
    )
    placement = (
        jnp.arange(HEADS, dtype=jnp.int32)[None, :] == heads_here[:, None]
    ).astype(jnp.float32)
    gate_local = jnp.sum(placement * gate_logit[None, :], axis=1)
    share = jax.nn.sigmoid(gate_local)
    piece_first = [piece_start[m, 0] - lax.axis_index("seg") * SEG_LEN for m in micros]

    def halves(*weights):
        return jnp.concatenate([column_half(w, group) for w in weights], axis=1)

    def other_halves(*weights):
        return jnp.concatenate([column_half(w, 1 - group) for w in weights], axis=1)

    bits = tok_bits()
    here = lax.axis_index("tok")
    order = tok_order(bits)
    here = here.astype(jnp.int32)[None]
    spots = jnp.array(order, jnp.int32) ^ here
    in_turn = jnp.arange(2 * len(order), dtype=jnp.int32)

    pair_weights = (query_weight, key_weight)
    pair_mine = seg_gather(line(halves, *pair_weights))
    normed_a = line(
        lambda x: root_norm(x.astype(jnp.float32), attend_gain).astype(jnp.bfloat16), hidden_in
    )
    attend_pieces = FirstPiece(normed_a, bits)
    cot_swapped = grp_swap(cotangent)
    value_mine = seg_gather(line(halves, value_weight))
    out_mine = seg_gather(line(halves, out_weight))
    feed_mine = seg_gather(line(halves, gate_weight, up_weight))
    down_mine = seg_gather(line(halves, down_weight))
    pair_other = line(other_halves, *pair_weights)
    value_other = line(other_halves, value_weight)
    out_other = line(other_halves, out_weight)
    cot_swapped = line.hold(cot_swapped)
    attend_pieces = attend_pieces.rest(line)
    cot_pieces = FirstPiece(line.hold(cotangent), bits)
    pair_got = grp_swap(line(other_segments, pair_mine))
    gathered_a = line(
        lambda *p: place(p, order, here),
        *[attend_pieces[at] for at in order],
    )
    gathered_a = [gathered_a[m * SEG_LEN : (m + 1) * SEG_LEN] for m in micros]
    value_got = grp_swap(line(other_segments, value_mine))

    def project(g, *weights):
        return tuple(
            tuple(times(g[m], w).astype(jnp.bfloat16) for m in micros) for w in weights
        )

    query_full, key_full = line(lambda *a: with_other(*a, 2), pair_mine, pair_got, pair_other)
    queries, key_rows = line(project, gathered_a, query_full, key_full)
    cot_pieces = cot_pieces.rest(line)
    cot_far = FirstPiece(cot_swapped, bits)
    (value_full,) = line(lambda *a: with_other(*a, 1), value_mine, value_got, value_other)
    (values,) = line(project, gathered_a, value_full)
    out_got = grp_swap(line(other_segments, out_mine))

    contrib, count_k = zip(*[line(features, key_rows[m], values[m]) for m in micros])
    arrived = seg_send(jnp.concatenate(contrib), jnp.concatenate(count_k), 1)
    local = [line(local_attention, queries[0], key_rows[0], values[0], piece_first[0])]
    (out_full,) = line(lambda *a: with_other(*a, 1), out_mine, out_got, out_other)
    cot_far = cot_far.rest(line)
    memory, norm_mem = line(seg_sum, arrived)
    memory = [memory[m * head_local : (m + 1) * head_local] for m in micros]
    norm_mem = [norm_mem[m * head_local : (m + 1) * head_local] for m in micros]
    mixes = []
    attended = []

    def mixed_rows(m):
        mixes.append(line(mixing, queries[m], local[m][0], memory[m], norm_mem[m], share))
        return line(lambda a, w: products_cut([a], [w], spots), mixes[m], out_full)

    for m in micros:
        if m > 0:
            local.append(line(local_attention, queries[m], key_rows[m], values[m], piece_first[m]))
        cut = mixed_rows(m)
        if m > 0:
            cut, attended[m - 1].terms = line.hold((cut, attended[m - 1].terms))
        attended.append(Scatter(*cut))
        attended[m].go_on(line)

    def after_attention(x, terms):
        resid = x.astype(jnp.float32) + total_of(terms)
        return (resid, root_norm(resid, feed_gain).astype(jnp.bfloat16))

    resid = []
    feed_pieces = []
    for m in micros:
        rows_m, normed_f = line(after_attention, hidden_in[m], attended[m].terms)
        resid.append(rows_m)
        over_tok = None
        if m + 1 < count:
            over_tok, attended[m + 1].terms = line.hold((normed_f[None], attended[m + 1].terms))
        feed_pieces.append(BothGroups(normed_f[None], bits, over_tok))
    for pieces in feed_pieces:
        pieces.go_on(line)
    feed_mine = line.hold(feed_mine)

    def interleaved(own, far):
        return [pieces[at] for at in order for pieces in (own, far)]

    feed_in = []
    products = []
    inner_act = []
    for m in micros:
        rows_m, both, inner = line(
            lambda w, *p: feed_forward(p, 0, w), feed_mine, *interleaved(*feed_pieces[m].finish(line))
        )
        feed_in.append(rows_m)
        products.append(both)
        inner_act.append(inner)

    cot_all = []
    grad_products = []
    grad_normed = []

    def backward(m):
        rows_m, grads = line(
            lambda w, both, *p: feed_backward(p, m, w, both),
            down_mine,
            products[m],
            *interleaved(cot_pieces, cot_far),
        )
        cot_all.append(rows_m)
        grad_products.append(grads)

    def backward_rows(m):
        return line(lambda a, w: products_cut([a], [w], in_turn), grad_products[m], feed_mine)

    def own_and_far(terms):
        total = total_of(terms)
        half = total.shape[0] // 2
        return (total[:half], total[half:].astype(jnp.bfloat16))

    def after_feed_grad(rows_m, own, far, cot):
        unused_norm, pull = jax.vjp(root_norm, rows_m, feed_gain)
        grad_norm, gain_part = pull(added(own, far))
        grad_resid = cot.astype(jnp.float32) + grad_norm
        return (grad_resid, gain_part, grad_resid.astype(jnp.bfloat16))

    grad_parts = []
    grad_resid = []
    feed_gain_parts = []
    att_pieces = []

    def finish_rows(m):
        own, far = line(own_and_far, grad_normed[m].terms)
        grad_parts.append((own, grp_swap(far)))

    def finish_feed(m):
        rows_m, gain_part, low = line(after_feed_grad, resid[m], *grad_parts[m], cotangent[m])
        grad_resid.append(rows_m)
        feed_gain_parts.append(gain_part)
        att_pieces.append(FirstPiece(low[None], bits))

    feed_out = []

    def feed_result(m):
        return line(lambda a, w: products_cut([a], [w], in_turn), inner_act[m], down_mine)

    backward(0)
    grad_normed.append(Scatter(*backward_rows(0)))
    backward(1)
    grad_normed[0].go_on(line)
    down_raw = line(lambda a, b: grad_product(a, [b]), cot_all, inner_act)
    cut = backward_rows(1)
    down_raw, cut, grad_normed[0].terms = line.hold((down_raw, cut, grad_normed[0].terms))
    grad_normed.append(Scatter(*cut))
    down_grad = seg_scatter(down_raw)
    finish_rows(0)
    grad_normed[1].go_on(line)
    feed_raw = line(lambda a, b: grad_product(a, [b]), feed_in, grad_products)
    feed_raw, grad_normed[1].terms, grad_parts[0] = line.hold(
        (feed_raw, grad_normed[1].terms, grad_parts[0])
    )
    feed_grad = seg_scatter(feed_raw)
    finish_rows(1)
    finish_feed(0)
    cut = feed_result(0)
    cut, grad_parts[1], att_pieces[0].got = line.hold((cut, grad_parts[1], att_pieces[0].got))
    finish_feed(1)
    att_pieces[0] = att_pieces[0].rest(line)
    feed_out.append(Scatter(*cut))
    down_grad = line.hold(down_grad)
    down_rest = grp_swap(down_grad)

    grad_att = []
    mem_back = []
    for m in micros:
        if m > 0:
            feed_out[m - 1].go_on(line)
            cut = feed_result(m)
            att_pieces[m] = att_pieces[m].rest(line)
            feed_out.append(Scatter(*line.hold(cut)))
        grad_att.append(
            line(lambda *p: place(p, order, here), *[att_pieces[m][at] for at in order])
        )
        mem_back.append(
            line(
                memory_backward,
                grad_att[m],
                out_full,
                queries[m],
                local[m][0],
                memory[m],
                norm_mem[m],
                share,
            )
        )
    logit_parts, grad_local, grad_query, grad_memory, grad_norm_mem = zip(*mem_back)
    back_arrived = seg_send(jnp.concatenate(grad_memory), jnp.concatenate(grad_norm_mem), -1)
    out_far = grp_swap(line(lambda a, b: grad_product(a, [b], 1), grad_att, mixes))
    feed_out[-1].go_on(line)
    local_back = []

    def local_grad(m):
        local_back.append(
            line(
                local_backward,
                queries[m],
                key_rows[m],
                values[m],
                local[m][1],
                grad_local[m],
                grad_query[m],
                piece_first[m],
            )
        )

    local_grad(0)
    down_out = line(whole_columns, down_grad, down_rest)
    local_grad(1)
    query_low, key_sums, value_sums = zip(*local_back)
    feed_parts = []
    for m in micros:
        own, far = line(own_and_far, feed_out[m].terms)
        feed_parts.append((own, grp_swap(far)))
    query_raw = line(lambda a, b: grad_product(a, [b]), gathered_a, query_low)
    grad_contrib, grad_count = line(seg_sum, back_arrived)
    out_raw = line(lambda a, b, far: grad_product(a, [b], 0, far), grad_att, mixes, out_far)
    feed_grad, out_raw = line.hold((feed_grad, out_raw))
    feed_half = gate_weight.shape[1] // 2
    gate_grad, up_grad = (feed_grad[:, :feed_half], feed_grad[:, feed_half:])
    gate_rest = grp_swap(gate_grad)
    out_grad = seg_scatter(out_raw)
    key_low, value_low = zip(
        *[
            line(
                with_memory,
                key_rows[m],
                values[m],
                key_sums[m],
                value_sums[m],
                grad_contrib[m * head_local : (m + 1) * head_local],
                grad_count[m * head_local : (m + 1) * head_local],
            )
            for m in micros
        ]
    )
    pair_far = grp_swap(
        line(lambda a, c, d: grad_product(a, [c, d], 1), gathered_a, key_low, value_low)
    )
    query_sum = seg_scatter(query_raw)
    grad_normed_a = []
    for m in micros:
        grad_normed_a.append(
            Scatter(
                *line(
                    lambda a, b, c, wa, wb, wc: products_cut([a, b, c], [wa, wb, wc], spots),
                    query_low[m],
                    key_low[m],
                    value_low[m],
                    query_full,
                    key_full,
                    value_full,
                )
            )
        )
    pair_far, out_grad = line.hold((pair_far, out_grad))
    pair_raw = line(
        lambda far, a, c, d: grad_product(a, [c, d], 0, far),
        pair_far,
        gathered_a,
        key_low,
        value_low,
    )
    pair_grad = seg_scatter(pair_raw)
    up_rest = grp_swap(line.hold(up_grad))
    out_rest = grp_swap(out_grad)
    for m in micros:
        grad_normed_a[m].go_on(line)
    gate_out = line(whole_columns, gate_grad, gate_rest)

    def after_attend_grad(x, terms, grad, gain):
        unused_norm, pull = jax.vjp(root_norm, x.astype(jnp.float32), gain)
        grad_norm, gain_part = pull(total_of(terms))
        return ((grad + grad_norm).astype(jnp.bfloat16), gain_part)

    gain, line.token = (line.token, out_grad)
    input_rows = []
    attend_gain_parts = []
    for m in micros:
        grad_rows, gain_part = line(
            after_attend_grad, hidden_in[m], grad_normed_a[m].terms, grad_resid[m], gain
        )
        input_rows.append(grad_rows)
        attend_gain_parts.append(gain_part)
    feed_parts = line.hold(feed_parts)
    gate_logit_part = jnp.sum(sum(logit_parts), axis=(1, 2)) * share * (1.0 - share)
    gate_full_grad = jnp.sum(placement * gate_logit_part[:, None], axis=0)
    small = line(
        lambda a, b, c: jnp.concatenate([sum(a), sum(b), c])[None],
        attend_gain_parts,
        feed_gain_parts,
        gate_full_grad,
    )
    small_steps = [
        (axis, 1 << k)
        for axis in ("tok", "seg", "grp")
        for k in range(lax.axis_size(axis).bit_length() - 1)
    ]

    def add_small(small, axis, bit):
        size = lax.axis_size(axis)
        other = lax.ppermute(small, axis, [(k, k ^ bit) for k in range(size)])
        return line(jnp.add, small, other)

    for axis, bit in small_steps[:-3]:
        small = add_small(small, axis, bit)
    query_sum = line.hold(query_sum)
    query_rest = grp_swap(query_sum)
    pair_grad, small = line.hold((pair_grad, small))
    pair_rest = grp_swap(pair_grad)
    up_out = line(whole_columns, up_grad, up_rest)
    small = add_small(small, *small_steps[-3])
    output_rows = [
        line(
            lambda r, own, far: (r + added(own, far)).astype(jnp.bfloat16), resid[m], *feed_parts[m]
        )
        for m in micros
    ]
    small = add_small(small, *small_steps[-2])
    query_grad = line(whole_sum, query_sum, query_rest)
    small = add_small(small, *small_steps[-1])
    key_grad, value_grad = line(
        lambda a, b: tuple(
            whole_columns(*[part[:, k * half : (k + 1) * half] for part in (a, b)])
            for k in range(2)
        ),
        pair_grad,
        pair_rest,
    )
    out_out = whole_columns(line.token, out_rest)
    small_sums = (small[0, :width], small[0, width : 2 * width], small[0, 2 * width :])
    return (
        (jnp.stack(output_rows), jnp.stack(input_rows))
        + (query_grad, key_grad, value_grad)
        + (out_out, gate_out, up_out, down_out)
        + small_sums
    )


def solution(mesh):
    return jax.shard_map(
        body,
        mesh=mesh,
        in_specs=(
            P("grp", ("seg", "tok"), None),
            P("grp", ("seg", "tok"), None),
            P("grp", "seg"),
            P("seg", "tok"),
            P("seg", "tok"),
            P("seg", "tok"),
            P("seg", "tok"),
            P("seg", "tok"),
            P("seg", "tok"),
            P("seg", "tok"),
            P(),
            P(),
            P(),
        ),
        out_specs=(
            P("grp", ("seg", "tok"), None),
            P("grp", ("seg", "tok"), None),
            P("seg", "tok"),
            P("seg", "tok"),
            P("seg", "tok"),
            P("seg", "tok"),
            P("seg", "tok"),
            P("seg", "tok"),
            P("seg", "tok"),
            P(),
            P(),
            P(),
        ),
        check_vma=False,
    )
```

```python
import jax
import jax.numpy as jnp
from jax import lax
from jax.experimental import pallas as pl
from jax.experimental.pallas import tpu as pltpu
from jax.sharding import PartitionSpec as P

HEADS = 16
HEAD_DIM = 128
SEG_LEN = 1024
PIECE = 256
VMEM_BYTES = 60 * 1024 * 1024
MICRO = 2


EPS_NORM = 1e-05
MASKED_SCORE = -1e30


class Line:
    def __init__(self, token):
        self.token = token

    def hold(self, value):
        value, self.token = lax.optimization_barrier((value, self.token))
        return value

    def __call__(self, step, *inputs):
        return self.hold(step(*self.hold(inputs)))


def tok_bits():
    return [1 << k for k in range(lax.axis_size("tok").bit_length() - 1)]


def tok_swap(value, bit):
    count = lax.axis_size("tok")
    return lax.ppermute(value, "tok", [(k, k ^ bit) for k in range(count)])


def tok_at(bit):
    return jnp.where((lax.axis_index("tok") & bit) == 0, 0, 1)


def grp_swap(value):
    return lax.ppermute(value, "grp", [(0, 1), (1, 0)])


def tok_pieces(rows, bits):
    pieces = {0: rows}
    for bit in reversed(bits):
        for at in sorted(pieces):
            pieces[at | bit] = tok_swap(pieces[at], bit)
    return pieces


def joined(near, far, bit):
    return {**near, **{at | bit: piece for at, piece in far.items()}}


class BothGroups:
    def __init__(self, rows, bits, over_tok=None):
        self.low, self.high = (bits[:-1], bits[-1])
        self.tok_first = over_tok is not None
        self.rows = rows
        self.swapped = tok_swap(over_tok if self.tok_first else rows, self.high)
        self.got = grp_swap(rows)

    def go_on(self, line):
        if self.tok_first:
            self.swapped = line.hold(self.swapped)
            self.late = grp_swap(self.swapped)
        else:
            self.late = tok_swap(self.got, self.high)
        self.own = joined(
            tok_pieces(self.rows, self.low), tok_pieces(self.swapped, self.low), self.high
        )
        self.far = tok_pieces(self.got, self.low)

    def finish(self, line):
        late = tok_pieces(line.hold(self.late), self.low)
        return (self.own, joined(self.far, late, self.high))


class FirstPiece:
    def __init__(self, rows, bits):
        self.rows = rows
        self.bits = bits
        self.got = tok_swap(rows, bits[-1])

    def rest(self, line):
        pieces = {0: self.rows, self.bits[-1]: line.hold(self.got)}
        for bit in reversed(self.bits[:-1]):
            for at in sorted(pieces):
                pieces[at | bit] = tok_swap(pieces[at], bit)
        return pieces


def added(kept, got):
    return kept.astype(jnp.float32) + got.astype(jnp.float32)


class Scatter:
    def __init__(self, kept, sent):
        self.bits = tok_bits()
        self.terms = (kept, tok_swap(sent, self.bits[0]))

    def go_on(self, line):
        def cut(*terms):
            rows = terms[-1].shape[0]
            return sum(term[rows // 2 : rows].astype(jnp.float32) for term in terms).astype(
                jnp.bfloat16
            )

        for bit in self.bits[1:]:
            self.terms = self.terms + (tok_swap(line(cut, *self.terms), bit),)


def total_of(terms):
    rows = terms[-1].shape[0]
    return sum(term[:rows].astype(jnp.float32) for term in terms)


def tok_order(bits):
    order = [0]
    for bit in reversed(bits):
        order = order + [at | bit for at in order]
    return order


def kernel_params():
    return pltpu.CompilerParams(vmem_limit_bytes=VMEM_BYTES)


def kernel_cost(flops, *arrays):
    moved = sum(a.size * a.dtype.itemsize for a in arrays)
    return pl.CostEstimate(flops=flops, transcendentals=0, bytes_accessed=moved)


def any_space():
    return pl.BlockSpec(memory_space=pl.ANY)


def kept_block(shape):
    return pl.BlockSpec(shape, lambda *at: (0,) * len(shape), pipeline_mode=pl.Buffered(1))


def place(pieces, order, here):
    rows, width = pieces[0].shape[-2:]
    total = sum(p.shape[0] for p in pieces)

    def kernel(here_ref, *refs):
        *ins, out, held, arrive, leave = refs
        copies = []
        for mask, ref in zip(order, ins):
            for j in range(ref.shape[0]):
                at = len(copies)
                spot = j * len(order) + (here_ref[0] ^ mask)
                start = pl.multiple_of(spot * rows, rows)
                copies.append(
                    (
                        pltpu.make_async_copy(ref.at[j], held.at[at], arrive.at[at]),
                        pltpu.make_async_copy(
                            held.at[at], out.at[pl.ds(start, rows)], leave.at[at]
                        ),
                    )
                )
        for first, _ in copies:
            first.start()
        for first, then in copies:
            first.wait()
            then.start()
        for _, then in copies:
            then.wait()

    out = jax.ShapeDtypeStruct((total * rows, width), pieces[0].dtype)
    return pl.pallas_call(
        kernel,
        in_specs=[pl.BlockSpec(memory_space=pltpu.SMEM)] + [any_space()] * len(pieces),
        out_specs=any_space(),
        out_shape=out,
        scratch_shapes=[
            pltpu.VMEM((total, rows, width), pieces[0].dtype),
            pltpu.SemaphoreType.DMA((total,)),
            pltpu.SemaphoreType.DMA((total,)),
        ],
        compiler_params=kernel_params(),
        cost_estimate=kernel_cost(0, out, out),
    )(here, *pieces)


def over_pieces(pieces, which, extra, extra_specs, outs, compute, flops):
    rows, width = pieces[0].shape[-2:]
    total = rows * len(pieces)
    block = max(rows, min(512, total))
    each = block // rows

    def kernel(*refs):
        ins = refs[: len(pieces)]
        others = refs[len(pieces) : len(pieces) + len(extra)]
        results = refs[len(pieces) + len(extra) : -2]
        held, arrive = refs[-2:]
        step = pl.program_id(0)

        def copy(at, ref):
            return pltpu.make_async_copy(
                ref.at[which], held.at[pl.ds(at * rows, rows)], arrive.at[at]
            )

        @pl.when(step == 0)
        def start_all():
            for at, ref in enumerate(ins):
                copy(at, ref).start()

        for part in range(each):
            copy(step * each + part, ins[0]).wait()
        x = held[pl.ds(pl.multiple_of(step * block, block), block)]
        results[0][...] = x
        compute(x, others, results[1:])

    row_spec = lambda n: pl.BlockSpec((block, n), lambda i: (i, 0))
    shapes = [jax.ShapeDtypeStruct((total, n), jnp.bfloat16) for n in (width,) + tuple(outs)]
    return pl.pallas_call(
        kernel,
        grid=(total // block,),
        in_specs=[any_space()] * len(pieces) + [spec(row_spec) for spec in extra_specs],
        out_specs=[row_spec(s.shape[1]) for s in shapes],
        out_shape=shapes,
        scratch_shapes=[
            pltpu.VMEM((total, width), pieces[0].dtype),
            pltpu.SemaphoreType.DMA((len(pieces),)),
        ],
        compiler_params=kernel_params(),
        cost_estimate=kernel_cost(flops, *shapes, *extra),
    )(*pieces, *extra)


def feed_forward(pieces, which, weight):
    hidden = weight.shape[1] // 2
    total = len(pieces) * pieces[0].shape[-2]

    def compute(x, others, results):
        both = jnp.dot(x, others[0][...], preferred_element_type=jnp.float32)
        gate, up = (both[:, :hidden], both[:, hidden:])
        results[0][...] = both.astype(jnp.bfloat16)
        results[1][...] = (gate * jax.nn.sigmoid(gate) * up).astype(jnp.bfloat16)

    return over_pieces(
        pieces,
        which,
        (weight,),
        (lambda row_spec: kept_block(weight.shape),),
        (2 * hidden, hidden),
        compute,
        2 * total * weight.size,
    )


def feed_backward(pieces, which, weight, both):
    hidden = weight.shape[1]
    total = len(pieces) * pieces[0].shape[-2]

    def compute(x, others, results):
        grad = jnp.dot(x, others[0][...], preferred_element_type=jnp.float32)
        gate = others[1][:, :hidden].astype(jnp.float32)
        up = others[1][:, hidden:].astype(jnp.float32)
        sig = jax.nn.sigmoid(gate)
        results[0][:, :hidden] = (grad * up * sig * (1.0 + gate * (1.0 - sig))).astype(jnp.bfloat16)
        results[0][:, hidden:] = (grad * gate * sig).astype(jnp.bfloat16)

    return over_pieces(
        pieces,
        which,
        (weight, both),
        (lambda row_spec: kept_block(weight.shape), lambda row_spec: row_spec(2 * hidden)),
        (2 * hidden,),
        compute,
        2 * total * weight.size,
    )


def products_cut(lefts, weights, order):
    total, width = (lefts[0].shape[0], weights[0].shape[0])
    steps = order.shape[0]
    rows = total // steps
    half = steps // 2
    pairs = len(lefts)

    def kernel(order_ref, *refs):
        out = 0.0
        for left, weight in zip(refs[:pairs], refs[pairs : 2 * pairs]):
            out = out + lax.dot_general(
                left[...],
                weight[...],
                (((1,), (1,)), ((), ())),
                preferred_element_type=jnp.float32,
            )
        sent_ref, kept_ref = refs[2 * pairs :]
        step = pl.program_id(0)

        @pl.when(step < half)
        def first_part():
            sent_ref[...] = out.astype(jnp.bfloat16)

        @pl.when(step >= half)
        def second_part():
            kept_ref[...] = out.astype(jnp.bfloat16)

    part = jax.ShapeDtypeStruct((total // 2, width), jnp.bfloat16)
    sent, kept = pl.pallas_call(
        kernel,
        grid_spec=pltpu.PrefetchScalarGridSpec(
            num_scalar_prefetch=1,
            grid=(steps,),
            in_specs=[
                pl.BlockSpec(
                    (rows, left.shape[1]), lambda i, at: (at[lax.rem(i + half, steps)], 0)
                )
                for left in lefts
            ]
            + [kept_block(weight.shape) for weight in weights],
            out_specs=[
                pl.BlockSpec((rows, width), lambda i, at: (jnp.minimum(i, half - 1), 0)),
                pl.BlockSpec((rows, width), lambda i, at: (jnp.maximum(i - half, 0), 0)),
            ],
        ),
        out_shape=[part, part],
        compiler_params=kernel_params(),
        cost_estimate=kernel_cost(
            sum(2 * total * weight.size for weight in weights), part, part, *lefts, *weights
        ),
    )(order, *lefts, *weights)
    return (kept, sent)


def grad_product(rows_of, columns_of, which=None, far=None):
    sets = len(columns_of)
    count = len(rows_of)
    total, width = rows_of[0].shape
    columns = columns_of[0][0].shape[1]
    part, at = (columns, 0) if which is None else (columns // 2, which)
    block = 256
    narrow = part % 128 != 0

    def kernel(*refs):
        rows = refs[:count]
        for k in range(sets):
            out = 0.0
            for left, right in zip(rows, refs[count + k * count : count + (k + 1) * count]):
                right = right[:, at * part : (at + 1) * part] if narrow else right[...]
                out = out + lax.dot_general(
                    left[...],
                    right,
                    (((0,), (0,)), ((), ())),
                    preferred_element_type=jnp.float32,
                )
            cut = slice(k * part, (k + 1) * part)
            if far is not None:
                out = out + refs[-2][:, cut].astype(jnp.float32)
            refs[-1][:, cut] = out.astype(jnp.bfloat16)

    out = jax.ShapeDtypeStruct((width, sets * part), jnp.bfloat16)
    flat_columns = [c for columns_set in columns_of for c in columns_set]
    column_spec = pl.BlockSpec(
        (total, columns) if narrow else (total, part),
        lambda i: (0, 0 if narrow else at),
        pipeline_mode=pl.Buffered(1),
    )
    out_spec = pl.BlockSpec((block, sets * part), lambda i: (i, 0))
    extra = [] if far is None else [far]
    return pl.pallas_call(
        kernel,
        grid=(width // block,),
        in_specs=[pl.BlockSpec((total, block), lambda i: (0, i))] * count
        + [column_spec] * len(flat_columns)
        + [out_spec] * len(extra),
        out_specs=out_spec,
        out_shape=out,
        compiler_params=kernel_params(),
        cost_estimate=kernel_cost(
            2 * count * total * width * part * sets, out, *rows_of, *flat_columns
        ),
    )(*rows_of, *flat_columns, *extra)


def seg_send(value, counts, step):
    size = lax.axis_size("seg")
    packed = jnp.concatenate([value, counts], axis=1).astype(jnp.bfloat16)
    return [
        lax.ppermute(
            packed,
            "seg",
            [(k, k + step * far) for k in range(size) if 0 <= k + step * far < size],
        )
        for far in range(1, size)
    ]


def seg_sum(arrived):
    total = sum(part.astype(jnp.float32) for part in arrived)
    return (total[:, :-1], total[:, -1:])


def column_half(weight, which):
    half = weight.shape[1] // 2
    return lax.dynamic_slice_in_dim(weight, which * half, half, 1)


def seg_gather(value):
    return lax.all_gather(value, "seg", axis=0, tiled=True)


def other_segments(gathered):
    size, here = (lax.axis_size("seg"), lax.axis_index("seg"))
    rows = gathered.shape[0] // size
    return jnp.concatenate(
        [
            lax.dynamic_slice_in_dim(gathered, lax.rem(here + k, size) * rows, rows, 0)
            for k in range(1, size)
        ],
        axis=0,
    )


def with_other(mine, got, own, pieces):
    size = mine.shape[0] // own.shape[0]
    rows, half = (own.shape[0], own.shape[1] // pieces)
    here = lax.axis_index("seg").astype(jnp.int32)[None]

    def kernel(here_ref, mine_ref, got_ref, own_ref, *outs):
        is_own = pl.program_id(0) == here_ref[0]
        rest = jnp.where(is_own, own_ref[...], got_ref[...])
        for k, out in enumerate(outs):
            cut = slice(k * half, (k + 1) * half)
            out[:, :half] = mine_ref[:, cut]
            out[:, half:] = rest[:, cut]

    def got_block(i, at):
        return (jnp.minimum(lax.rem(i + size - at[0] - 1 + size, size), size - 2), 0)

    out = jax.ShapeDtypeStruct((mine.shape[0], 2 * half), mine.dtype)
    return pl.pallas_call(
        kernel,
        grid_spec=pltpu.PrefetchScalarGridSpec(
            num_scalar_prefetch=1,
            grid=(size,),
            in_specs=[
                pl.BlockSpec((rows, own.shape[1]), lambda i, at: (i, 0)),
                pl.BlockSpec((rows, own.shape[1]), got_block),
                pl.BlockSpec((rows, own.shape[1]), lambda i, at: (0, 0)),
            ],
            out_specs=[pl.BlockSpec((rows, 2 * half), lambda i, at: (i, 0))] * pieces,
        ),
        out_shape=[out] * pieces,
        compiler_params=kernel_params(),
        cost_estimate=kernel_cost(0, mine, mine, mine, mine),
    )(here, mine, got, own)


def seg_scatter(value):
    return lax.psum_scatter(value, "seg", scatter_dimension=0, tiled=True)


def whole_columns(own, rest):
    first = lax.axis_index("grp") == 0
    return jnp.where(
        first, jnp.concatenate([own, rest], axis=1), jnp.concatenate([rest, own], axis=1)
    ).astype(jnp.float32)


def whole_sum(own, far):
    half = own.shape[1] // 2
    turned = jnp.concatenate([far[:, half:], far[:, :half]], axis=1)
    total = added(own, turned)
    first = lax.axis_index("grp") == 0
    return jnp.where(first, total, jnp.concatenate([total[:, half:], total[:, :half]], axis=1))


def times(left, right):
    return jnp.dot(left, right, preferred_element_type=jnp.float32)


def times_rows(left, right):
    return jnp.einsum("tc,dc->td", left, right, preferred_element_type=jnp.float32)


def weight_grad(rows, columns):
    return jnp.einsum("td,tc->dc", rows, columns, preferred_element_type=jnp.float32)


def root_norm(values, gain):
    return values * lax.rsqrt(jnp.mean(values * values, -1, keepdims=True) + EPS_NORM) * gain


def positive_feature(values):
    return jnp.where(values > 0, values + 1.0, jnp.exp(jnp.where(values > 0, 0.0, values)))


def feature_slope(values):
    return jnp.where(values > 0, 1.0, jnp.exp(jnp.where(values > 0, 0.0, values)))


def dot_as(left, right, dims):
    return lax.dot_general(left, right, (dims, ((), ())), preferred_element_type=jnp.float32)


ROWS_COLUMNS = ((1,), (0,))
BY_COLUMNS = ((1,), (1,))
BY_ROWS = ((0,), (0,))


def head_call(kernel, ins, outs, flops, scratch=()):
    def spec(shape, kind):
        if kind == "smem":
            return pl.BlockSpec(memory_space=pltpu.SMEM)
        if kind == "all":
            return kept_block(shape)
        if kind == "columns":
            return pl.BlockSpec((shape[0], HEAD_DIM), lambda i: (0, i))
        return pl.BlockSpec((1,) + shape[1:], lambda i: (i, 0, 0))

    heads = [s.shape[0] for s, kind in outs if kind == "heads"] + [
        s.shape[1] // HEAD_DIM for s, kind in outs if kind == "columns"
    ]
    return pl.pallas_call(
        kernel,
        grid=(heads[0],),
        in_specs=[spec(a.shape, kind) for a, kind in ins],
        out_specs=[spec(s.shape, kind) for s, kind in outs],
        out_shape=[s for s, kind in outs],
        scratch_shapes=list(scratch),
        compiler_params=kernel_params(),
        cost_estimate=kernel_cost(
            flops, *[a for a, kind in ins if kind != "smem"], *[s for s, kind in outs]
        ),
    )(*[a for a, kind in ins])


def low_feature(values):
    return positive_feature(values.astype(jnp.float32)).astype(jnp.bfloat16)


def like(shape, dtype):
    return jax.ShapeDtypeStruct(shape, dtype)


def features(key_rows, values):
    heads = key_rows.shape[1] // HEAD_DIM

    def kernel(key_ref, value_ref, contrib_ref, count_ref):
        feat_k = low_feature(key_ref[...])
        contrib_ref[0] = dot_as(feat_k, value_ref[...], BY_ROWS)
        count_ref[0] = jnp.sum(feat_k.astype(jnp.float32), axis=0, keepdims=True)

    return head_call(
        kernel,
        [(key_rows, "columns"), (values, "columns")],
        [
            (like((heads, HEAD_DIM, HEAD_DIM), jnp.float32), "heads"),
            (like((heads, 1, HEAD_DIM), jnp.float32), "heads"),
        ],
        2 * SEG_LEN * heads * HEAD_DIM**2,
    )


def reach_of(at):
    return min(SEG_LEN, (at + 2) * PIECE)


def masked_scores(query_block, keys, at, piece_first):
    scores = dot_as(query_block, keys, BY_COLUMNS) * HEAD_DIM ** (-0.5)
    rows_at = at * PIECE + lax.broadcasted_iota(jnp.int32, scores.shape, 0)
    keys_at = lax.broadcasted_iota(jnp.int32, scores.shape, 1)
    row_in = (rows_at >= piece_first) & (rows_at < piece_first + PIECE)
    key_in = (keys_at >= piece_first) & (keys_at < piece_first + PIECE)
    return jnp.where((keys_at <= rows_at) | (row_in & key_in), scores, MASKED_SCORE)


def local_flops(heads, products):
    return products * 2 * heads * HEAD_DIM * PIECE * sum(reach_of(k) for k in range(SEG_LEN // PIECE))


def local_attention(queries, key_rows, values, piece_first):
    heads = queries.shape[1] // HEAD_DIM

    def kernel(first_ref, query_ref, key_ref, value_ref, out_ref, log_ref):
        first = first_ref[0]
        for at in range(SEG_LEN // PIECE):
            rows = slice(at * PIECE, (at + 1) * PIECE)
            reach = reach_of(at)
            scores = masked_scores(query_ref[rows, :], key_ref[:reach, :], at, first)
            peak = jnp.max(scores, axis=-1, keepdims=True)
            shifted = jnp.exp(scores - peak)
            total = jnp.sum(shifted, axis=-1, keepdims=True)
            probs = (shifted * (1.0 / total)).astype(jnp.bfloat16)
            out_ref[rows, :] = dot_as(probs, value_ref[:reach, :], ROWS_COLUMNS)
            log_ref[0, rows, :] = peak + jnp.log(total)

    return head_call(
        kernel,
        [
            (piece_first[None], "smem"),
            (queries, "columns"),
            (key_rows, "columns"),
            (values, "columns"),
        ],
        [
            (like(queries.shape, jnp.float32), "columns"),
            (like((heads, SEG_LEN, 1), jnp.float32), "heads"),
        ],
        local_flops(heads, 2),
    )


def recalled(feat_q, memory, norm_mem):
    numerator = dot_as(feat_q, memory.astype(jnp.bfloat16), ROWS_COLUMNS)
    denominator = 1.0 + jnp.sum(feat_q.astype(jnp.float32) * norm_mem, axis=-1, keepdims=True)
    return (numerator / denominator, denominator)


def mixing(queries, local_out, memory, norm_mem, share):
    heads = queries.shape[1] // HEAD_DIM

    def kernel(share_ref, query_ref, local_ref, memory_ref, norm_ref, out_ref):
        part = share_ref[pl.program_id(0)]
        recall, unused = recalled(low_feature(query_ref[...]), memory_ref[0], norm_ref[0])
        out_ref[...] = (part * recall + (1.0 - part) * local_ref[...]).astype(jnp.bfloat16)

    return head_call(
        kernel,
        [
            (share, "smem"),
            (queries, "columns"),
            (local_out, "columns"),
            (memory, "heads"),
            (norm_mem, "heads"),
        ],
        [(like(queries.shape, jnp.bfloat16), "columns")],
        2 * SEG_LEN * heads * HEAD_DIM**2,
    )[0]


def memory_backward(grad_att, out_full, queries, local_out, memory, norm_mem, share):
    heads = queries.shape[1] // HEAD_DIM

    def kernel(
        share_ref,
        grad_ref,
        weight_ref,
        query_ref,
        local_ref,
        memory_ref,
        norm_ref,
        logit_ref,
        grad_local_ref,
        grad_query_ref,
        grad_memory_ref,
        grad_norm_ref,
    ):
        part = share_ref[pl.program_id(0)]
        queries_f = query_ref[...].astype(jnp.float32)
        feat_q = low_feature(query_ref[...])
        recall, denominator = recalled(feat_q, memory_ref[0], norm_ref[0])
        grad_mixed = dot_as(grad_ref[...], weight_ref[...], ROWS_COLUMNS)
        logit_ref[0] = jnp.sum(grad_mixed * (recall - local_ref[...]), axis=0, keepdims=True)
        grad_local_ref[...] = ((1.0 - part) * grad_mixed).astype(jnp.bfloat16)
        grad_scaled = part * grad_mixed / denominator
        grad_numer = grad_scaled.astype(jnp.bfloat16)
        grad_denom = -jnp.sum(grad_scaled * recall, axis=-1, keepdims=True)
        grad_feat = (
            dot_as(grad_numer, memory_ref[0].astype(jnp.bfloat16), BY_COLUMNS)
            + grad_denom * norm_ref[0]
        )
        grad_query_ref[...] = grad_feat * feature_slope(queries_f)
        grad_memory_ref[0] = dot_as(feat_q, grad_numer, BY_ROWS)
        grad_norm_ref[0] = jnp.sum(feat_q.astype(jnp.float32) * grad_denom, axis=0, keepdims=True)

    square = like((heads, HEAD_DIM, HEAD_DIM), jnp.float32)
    row = like((heads, 1, HEAD_DIM), jnp.float32)
    return head_call(
        kernel,
        [
            (share, "smem"),
            (grad_att, "all"),
            (out_full, "columns"),
            (queries, "columns"),
            (local_out, "columns"),
            (memory, "heads"),
            (norm_mem, "heads"),
        ],
        [
            (row, "heads"),
            (like(queries.shape, jnp.bfloat16), "columns"),
            (like(queries.shape, jnp.float32), "columns"),
            (square, "heads"),
            (row, "heads"),
        ],
        2 * grad_att.size * queries.shape[1] + 6 * SEG_LEN * heads * HEAD_DIM**2,
    )


def local_backward(queries, key_rows, values, log_totals, grad_local, grad_query, piece_first):
    heads = queries.shape[1] // HEAD_DIM

    def kernel(
        first_ref,
        query_ref,
        key_ref,
        value_ref,
        log_ref,
        local_ref,
        memory_ref,
        query_out,
        key_out,
        value_out,
    ):
        first = first_ref[0]
        scale = HEAD_DIM ** (-0.5)
        for at in range(SEG_LEN // PIECE):
            rows = slice(at * PIECE, (at + 1) * PIECE)
            reach = reach_of(at)
            known = reach_of(at - 1) if at > 0 else 0
            query_block = query_ref[rows, :]
            local_block = local_ref[rows, :]
            scores = masked_scores(query_block, key_ref[:reach, :], at, first)
            probs = jnp.exp(scores - log_ref[0, rows, :])
            grad_probs = dot_as(local_block, value_ref[:reach, :], BY_COLUMNS)
            weighed = probs * grad_probs
            mean = jnp.sum(weighed, axis=-1, keepdims=True)
            grad_scores = (weighed - probs * mean).astype(jnp.bfloat16)
            query_out[rows, :] = (
                dot_as(grad_scores, key_ref[:reach, :], ROWS_COLUMNS) * scale + memory_ref[rows, :]
            ).astype(jnp.bfloat16)
            for out, part in (
                (key_out, dot_as(grad_scores, query_block, BY_ROWS) * scale),
                (value_out, dot_as(probs.astype(jnp.bfloat16), local_block, BY_ROWS)),
            ):
                if known > 0:
                    out[:known, :] += part[:known]
                if known < reach:
                    out[known:reach, :] = part[known:]

    wide = (like(queries.shape, jnp.float32), "columns")
    return head_call(
        kernel,
        [
            (piece_first[None], "smem"),
            (queries, "columns"),
            (key_rows, "columns"),
            (values, "columns"),
            (log_totals, "heads"),
            (grad_local, "columns"),
            (grad_query, "columns"),
        ],
        [(like(queries.shape, jnp.bfloat16), "columns"), wide, wide],
        local_flops(heads, 5),
    )


def with_memory(key_rows, values, key_sum, value_sum, grad_contrib, grad_count):
    heads = key_rows.shape[1] // HEAD_DIM

    def kernel(key_ref, value_ref, key_sum, value_sum, contrib_ref, count_ref, key_out, value_out):
        keys = key_ref[...]
        contrib = contrib_ref[0].astype(jnp.bfloat16)
        grad_feat = dot_as(value_ref[...], contrib, BY_COLUMNS) + count_ref[0]
        slope = feature_slope(keys.astype(jnp.float32))
        key_out[...] = (key_sum[...] + grad_feat * slope).astype(jnp.bfloat16)
        value_out[...] = (
            value_sum[...] + dot_as(low_feature(keys), contrib, ROWS_COLUMNS)
        ).astype(jnp.bfloat16)

    out = (like(key_rows.shape, jnp.bfloat16), "columns")
    return head_call(
        kernel,
        [
            (key_rows, "columns"),
            (values, "columns"),
            (key_sum, "columns"),
            (value_sum, "columns"),
            (grad_contrib, "heads"),
            (grad_count, "heads"),
        ],
        [out, out],
        4 * SEG_LEN * heads * HEAD_DIM**2,
    )


def body(
    hidden_in,
    cotangent,
    piece_start,
    query_weight,
    key_weight,
    value_weight,
    out_weight,
    gate_weight,
    up_weight,
    down_weight,
    attend_gain,
    feed_gain,
    gate_logit,
):
    line = Line(attend_gain)
    group = lax.axis_index("grp")
    count, rows, width = hidden_in.shape
    micros = range(count)
    columns = query_weight.shape[1]
    half = columns // 2
    head_local = columns // HEAD_DIM
    head_turn = group * (head_local // 2)
    heads_here = lax.axis_index("tok") * head_local + lax.rem(
        jnp.arange(head_local, dtype=jnp.int32) + head_turn, head_local
    )
    placement = (
        jnp.arange(HEADS, dtype=jnp.int32)[None, :] == heads_here[:, None]
    ).astype(jnp.float32)
    gate_local = jnp.sum(placement * gate_logit[None, :], axis=1)
    share = jax.nn.sigmoid(gate_local)
    piece_first = [piece_start[m, 0] - lax.axis_index("seg") * SEG_LEN for m in micros]

    def halves(*weights):
        return jnp.concatenate([column_half(w, group) for w in weights], axis=1)

    def other_halves(*weights):
        return jnp.concatenate([column_half(w, 1 - group) for w in weights], axis=1)

    bits = tok_bits()
    here = lax.axis_index("tok")
    order = tok_order(bits)
    here = here.astype(jnp.int32)[None]
    spots = jnp.array(order, jnp.int32) ^ here
    in_turn = jnp.arange(2 * len(order), dtype=jnp.int32)

    pair_weights = (query_weight, key_weight)
    pair_mine = seg_gather(line(halves, *pair_weights))
    normed_a = line(
        lambda x: root_norm(x.astype(jnp.float32), attend_gain).astype(jnp.bfloat16), hidden_in
    )
    attend_pieces = FirstPiece(normed_a, bits)
    cot_swapped = grp_swap(cotangent)
    value_mine = seg_gather(line(halves, value_weight))
    out_mine = seg_gather(line(halves, out_weight))
    feed_mine = seg_gather(line(halves, gate_weight, up_weight))
    down_mine = seg_gather(line(halves, down_weight))
    pair_other = line(other_halves, *pair_weights)
    value_other = line(other_halves, value_weight)
    out_other = line(other_halves, out_weight)
    cot_swapped = line.hold(cot_swapped)
    attend_pieces = attend_pieces.rest(line)
    cot_pieces = FirstPiece(line.hold(cotangent), bits)
    pair_got = grp_swap(line(other_segments, pair_mine))
    gathered_a = line(
        lambda *p: place(p, order, here),
        *[attend_pieces[at] for at in order],
    )
    gathered_a = [gathered_a[m * SEG_LEN : (m + 1) * SEG_LEN] for m in micros]
    value_got = grp_swap(line(other_segments, value_mine))

    def project(g, *weights):
        return tuple(
            tuple(times(g[m], w).astype(jnp.bfloat16) for m in micros) for w in weights
        )

    query_full, key_full = line(lambda *a: with_other(*a, 2), pair_mine, pair_got, pair_other)
    queries, key_rows = line(project, gathered_a, query_full, key_full)
    cot_pieces = cot_pieces.rest(line)
    cot_far = FirstPiece(cot_swapped, bits)
    (value_full,) = line(lambda *a: with_other(*a, 1), value_mine, value_got, value_other)
    (values,) = line(project, gathered_a, value_full)
    out_got = grp_swap(line(other_segments, out_mine))

    contrib, count_k = zip(*[line(features, key_rows[m], values[m]) for m in micros])
    arrived = seg_send(jnp.concatenate(contrib), jnp.concatenate(count_k), 1)
    local = [line(local_attention, queries[0], key_rows[0], values[0], piece_first[0])]
    (out_full,) = line(lambda *a: with_other(*a, 1), out_mine, out_got, out_other)
    cot_far = cot_far.rest(line)
    memory, norm_mem = line(seg_sum, arrived)
    memory = [memory[m * head_local : (m + 1) * head_local] for m in micros]
    norm_mem = [norm_mem[m * head_local : (m + 1) * head_local] for m in micros]
    mixes = []
    attended = []

    def mixed_rows(m):
        mixes.append(line(mixing, queries[m], local[m][0], memory[m], norm_mem[m], share))
        return line(lambda a, w: products_cut([a], [w], spots), mixes[m], out_full)

    for m in micros:
        if m > 0:
            local.append(line(local_attention, queries[m], key_rows[m], values[m], piece_first[m]))
        cut = mixed_rows(m)
        if m > 0:
            cut, attended[m - 1].terms = line.hold((cut, attended[m - 1].terms))
        attended.append(Scatter(*cut))
        attended[m].go_on(line)

    def after_attention(x, terms):
        resid = x.astype(jnp.float32) + total_of(terms)
        return (resid, root_norm(resid, feed_gain).astype(jnp.bfloat16))

    resid = []
    feed_pieces = []
    for m in micros:
        rows_m, normed_f = line(after_attention, hidden_in[m], attended[m].terms)
        resid.append(rows_m)
        over_tok = None
        if m + 1 < count:
            over_tok, attended[m + 1].terms = line.hold((normed_f[None], attended[m + 1].terms))
        feed_pieces.append(BothGroups(normed_f[None], bits, over_tok))
    for pieces in feed_pieces:
        pieces.go_on(line)
    feed_mine = line.hold(feed_mine)

    def interleaved(own, far):
        return [pieces[at] for at in order for pieces in (own, far)]

    feed_in = []
    products = []
    inner_act = []
    for m in micros:
        rows_m, both, inner = line(
            lambda w, *p: feed_forward(p, 0, w), feed_mine, *interleaved(*feed_pieces[m].finish(line))
        )
        feed_in.append(rows_m)
        products.append(both)
        inner_act.append(inner)

    cot_all = []
    grad_products = []
    grad_normed = []

    def backward(m):
        rows_m, grads = line(
            lambda w, both, *p: feed_backward(p, m, w, both),
            down_mine,
            products[m],
            *interleaved(cot_pieces, cot_far),
        )
        cot_all.append(rows_m)
        grad_products.append(grads)

    def backward_rows(m):
        return line(lambda a, w: products_cut([a], [w], in_turn), grad_products[m], feed_mine)

    def own_and_far(terms):
        total = total_of(terms)
        half = total.shape[0] // 2
        return (total[:half], total[half:].astype(jnp.bfloat16))

    def after_feed_grad(rows_m, own, far, cot):
        unused_norm, pull = jax.vjp(root_norm, rows_m, feed_gain)
        grad_norm, gain_part = pull(added(own, far))
        grad_resid = cot.astype(jnp.float32) + grad_norm
        return (grad_resid, gain_part, grad_resid.astype(jnp.bfloat16))

    grad_parts = []
    grad_resid = []
    feed_gain_parts = []
    att_pieces = []

    def finish_rows(m):
        own, far = line(own_and_far, grad_normed[m].terms)
        grad_parts.append((own, grp_swap(far)))

    def finish_feed(m):
        rows_m, gain_part, low = line(after_feed_grad, resid[m], *grad_parts[m], cotangent[m])
        grad_resid.append(rows_m)
        feed_gain_parts.append(gain_part)
        att_pieces.append(FirstPiece(low[None], bits))

    feed_out = []

    def feed_result(m):
        return line(lambda a, w: products_cut([a], [w], in_turn), inner_act[m], down_mine)

    backward(0)
    grad_normed.append(Scatter(*backward_rows(0)))
    backward(1)
    grad_normed[0].go_on(line)
    down_raw = line(lambda a, b: grad_product(a, [b]), cot_all, inner_act)
    cut = backward_rows(1)
    down_raw, cut, grad_normed[0].terms = line.hold((down_raw, cut, grad_normed[0].terms))
    grad_normed.append(Scatter(*cut))
    down_grad = seg_scatter(down_raw)
    finish_rows(0)
    grad_normed[1].go_on(line)
    feed_raw = line(lambda a, b: grad_product(a, [b]), feed_in, grad_products)
    feed_raw, grad_normed[1].terms, grad_parts[0] = line.hold(
        (feed_raw, grad_normed[1].terms, grad_parts[0])
    )
    feed_grad = seg_scatter(feed_raw)
    finish_rows(1)
    finish_feed(0)
    cut = feed_result(0)
    cut, grad_parts[1], att_pieces[0].got = line.hold((cut, grad_parts[1], att_pieces[0].got))
    finish_feed(1)
    att_pieces[0] = att_pieces[0].rest(line)
    feed_out.append(Scatter(*cut))
    down_grad = line.hold(down_grad)
    down_rest = grp_swap(down_grad)

    grad_att = []
    mem_back = []
    for m in micros:
        if m > 0:
            feed_out[m - 1].go_on(line)
            cut = feed_result(m)
            att_pieces[m] = att_pieces[m].rest(line)
            feed_out.append(Scatter(*line.hold(cut)))
        grad_att.append(
            line(lambda *p: place(p, order, here), *[att_pieces[m][at] for at in order])
        )
        mem_back.append(
            line(
                memory_backward,
                grad_att[m],
                out_full,
                queries[m],
                local[m][0],
                memory[m],
                norm_mem[m],
                share,
            )
        )
    logit_parts, grad_local, grad_query, grad_memory, grad_norm_mem = zip(*mem_back)
    back_arrived = seg_send(jnp.concatenate(grad_memory), jnp.concatenate(grad_norm_mem), -1)
    out_far = grp_swap(line(lambda a, b: grad_product(a, [b], 1), grad_att, mixes))
    feed_out[-1].go_on(line)
    local_back = []

    def local_grad(m):
        local_back.append(
            line(
                local_backward,
                queries[m],
                key_rows[m],
                values[m],
                local[m][1],
                grad_local[m],
                grad_query[m],
                piece_first[m],
            )
        )

    local_grad(0)
    out_far = line.hold(out_far)
    down_out = line(whole_columns, down_grad, down_rest)
    local_grad(1)
    query_low, key_sums, value_sums = zip(*local_back)
    feed_parts = []
    for m in micros:
        own, far = line(own_and_far, feed_out[m].terms)
        feed_parts.append((own, grp_swap(far)))
    query_raw = line(lambda a, b: grad_product(a, [b]), gathered_a, query_low)
    feed_parts[0], grad_contrib, grad_count = line.hold(
        (feed_parts[0],) + line(seg_sum, back_arrived)
    )
    out_raw = line(lambda a, b, far: grad_product(a, [b], 0, far), grad_att, mixes, out_far)
    feed_grad, out_raw = line.hold((feed_grad, out_raw))
    feed_half = gate_weight.shape[1] // 2
    gate_grad, up_grad = (feed_grad[:, :feed_half], feed_grad[:, feed_half:])
    gate_rest = grp_swap(gate_grad)
    out_grad = seg_scatter(out_raw)
    key_low, value_low = zip(
        *[
            line(
                with_memory,
                key_rows[m],
                values[m],
                key_sums[m],
                value_sums[m],
                grad_contrib[m * head_local : (m + 1) * head_local],
                grad_count[m * head_local : (m + 1) * head_local],
            )
            for m in micros
        ]
    )
    pair_far = line(lambda a, c, d: grad_product(a, [c, d], 1), gathered_a, key_low, value_low)
    pair_far, gate_rest = line.hold((pair_far, gate_rest))
    pair_far = grp_swap(pair_far)
    query_sum = seg_scatter(query_raw)
    grad_normed_a = []
    for m in micros:
        grad_normed_a.append(
            Scatter(
                *line(
                    lambda a, b, c, wa, wb, wc: products_cut([a, b, c], [wa, wb, wc], spots),
                    query_low[m],
                    key_low[m],
                    value_low[m],
                    query_full,
                    key_full,
                    value_full,
                )
            )
        )
    pair_far, out_grad = line.hold((pair_far, out_grad))
    pair_raw = line(
        lambda far, a, c, d: grad_product(a, [c, d], 0, far),
        pair_far,
        gathered_a,
        key_low,
        value_low,
    )
    pair_grad = seg_scatter(pair_raw)
    up_rest = grp_swap(line.hold(up_grad))
    out_rest = grp_swap(out_grad)
    for m in micros:
        grad_normed_a[m].go_on(line)
    gate_out = line(whole_columns, gate_grad, gate_rest)

    def after_attend_grad(x, terms, grad, gain):
        unused_norm, pull = jax.vjp(root_norm, x.astype(jnp.float32), gain)
        grad_norm, gain_part = pull(total_of(terms))
        return ((grad + grad_norm).astype(jnp.bfloat16), gain_part)

    gain, line.token = (line.token, out_grad)
    input_rows = []
    attend_gain_parts = []
    for m in micros:
        grad_rows, gain_part = line(
            after_attend_grad, hidden_in[m], grad_normed_a[m].terms, grad_resid[m], gain
        )
        input_rows.append(grad_rows)
        attend_gain_parts.append(gain_part)
    feed_parts = line.hold(feed_parts)
    gate_logit_part = jnp.sum(sum(logit_parts), axis=(1, 2)) * share * (1.0 - share)
    gate_full_grad = jnp.sum(placement * gate_logit_part[:, None], axis=0)
    small = line(
        lambda a, b, c: jnp.concatenate([sum(a), sum(b), c])[None],
        attend_gain_parts,
        feed_gain_parts,
        gate_full_grad,
    )
    small_steps = [
        (axis, 1 << k)
        for axis in ("tok", "seg", "grp")
        for k in range(lax.axis_size(axis).bit_length() - 1)
    ]

    def add_small(small, axis, bit):
        size = lax.axis_size(axis)
        other = lax.ppermute(small, axis, [(k, k ^ bit) for k in range(size)])
        return line(jnp.add, small, other)

    for axis, bit in small_steps[:-3]:
        small = add_small(small, axis, bit)
    query_sum = line.hold(query_sum)
    query_rest = grp_swap(query_sum)
    pair_grad, small = line.hold((pair_grad, small))
    pair_rest = grp_swap(pair_grad)
    up_out = line(whole_columns, up_grad, up_rest)
    small = add_small(small, *small_steps[-3])
    output_rows = [
        line(
            lambda r, own, far: (r + added(own, far)).astype(jnp.bfloat16), resid[m], *feed_parts[m]
        )
        for m in micros
    ]
    small = add_small(small, *small_steps[-2])
    query_grad = line(whole_sum, query_sum, query_rest)
    small = add_small(small, *small_steps[-1])
    key_grad, value_grad = line(
        lambda a, b: tuple(
            whole_columns(*[part[:, k * half : (k + 1) * half] for part in (a, b)])
            for k in range(2)
        ),
        pair_grad,
        pair_rest,
    )
    out_out = whole_columns(line.token, out_rest)
    small_sums = (small[0, :width], small[0, width : 2 * width], small[0, 2 * width :])
    return (
        (jnp.stack(output_rows), jnp.stack(input_rows))
        + (query_grad, key_grad, value_grad)
        + (out_out, gate_out, up_out, down_out)
        + small_sums
    )


def solution(mesh):
    return jax.shard_map(
        body,
        mesh=mesh,
        in_specs=(
            P("grp", ("seg", "tok"), None),
            P("grp", ("seg", "tok"), None),
            P("grp", "seg"),
            P("seg", "tok"),
            P("seg", "tok"),
            P("seg", "tok"),
            P("seg", "tok"),
            P("seg", "tok"),
            P("seg", "tok"),
            P("seg", "tok"),
            P(),
            P(),
            P(),
        ),
        out_specs=(
            P("grp", ("seg", "tok"), None),
            P("grp", ("seg", "tok"), None),
            P("seg", "tok"),
            P("seg", "tok"),
            P("seg", "tok"),
            P("seg", "tok"),
            P("seg", "tok"),
            P("seg", "tok"),
            P("seg", "tok"),
            P(),
            P(),
            P(),
        ),
        check_vma=False,
    )
```

```python
import jax
import jax.numpy as jnp
from jax import lax
from jax.experimental import pallas as pl
from jax.experimental.pallas import tpu as pltpu
from jax.sharding import PartitionSpec as P

HEADS = 16
HEAD_DIM = 128
SEG_LEN = 1024
PIECE = 256
VMEM_BYTES = 60 * 1024 * 1024
MICRO = 2


EPS_NORM = 1e-05
MASKED_SCORE = -1e30


class Line:
    def __init__(self, token):
        self.token = token

    def hold(self, value):
        value, self.token = lax.optimization_barrier((value, self.token))
        return value

    def __call__(self, step, *inputs):
        return self.hold(step(*self.hold(inputs)))


def tok_bits():
    return [1 << k for k in range(lax.axis_size("tok").bit_length() - 1)]


def tok_swap(value, bit):
    count = lax.axis_size("tok")
    return lax.ppermute(value, "tok", [(k, k ^ bit) for k in range(count)])


def tok_at(bit):
    return jnp.where((lax.axis_index("tok") & bit) == 0, 0, 1)


def grp_swap(value):
    return lax.ppermute(value, "grp", [(0, 1), (1, 0)])


def tok_pieces(rows, bits):
    pieces = {0: rows}
    for bit in reversed(bits):
        for at in sorted(pieces):
            pieces[at | bit] = tok_swap(pieces[at], bit)
    return pieces


def joined(near, far, bit):
    return {**near, **{at | bit: piece for at, piece in far.items()}}


class BothGroups:
    def __init__(self, rows, bits, over_tok=None):
        self.low, self.high = (bits[:-1], bits[-1])
        self.tok_first = over_tok is not None
        self.rows = rows
        self.swapped = tok_swap(over_tok if self.tok_first else rows, self.high)
        self.got = grp_swap(rows)

    def go_on(self, line):
        if self.tok_first:
            self.swapped = line.hold(self.swapped)
            self.late = grp_swap(self.swapped)
        else:
            self.late = tok_swap(self.got, self.high)
        self.own = joined(
            tok_pieces(self.rows, self.low), tok_pieces(self.swapped, self.low), self.high
        )
        self.far = tok_pieces(self.got, self.low)

    def finish(self, line):
        late = tok_pieces(line.hold(self.late), self.low)
        return (self.own, joined(self.far, late, self.high))


class FirstPiece:
    def __init__(self, rows, bits):
        self.rows = rows
        self.bits = bits
        self.got = tok_swap(rows, bits[-1])

    def rest(self, line):
        pieces = {0: self.rows, self.bits[-1]: line.hold(self.got)}
        for bit in reversed(self.bits[:-1]):
            for at in sorted(pieces):
                pieces[at | bit] = tok_swap(pieces[at], bit)
        return pieces


def added(kept, got):
    return kept.astype(jnp.float32) + got.astype(jnp.float32)


class Scatter:
    def __init__(self, kept, sent):
        self.bits = tok_bits()
        self.terms = (kept, tok_swap(sent, self.bits[0]))

    def go_on(self, line):
        def cut(*terms):
            rows = terms[-1].shape[0]
            return sum(term[rows // 2 : rows].astype(jnp.float32) for term in terms).astype(
                jnp.bfloat16
            )

        for bit in self.bits[1:]:
            self.terms = self.terms + (tok_swap(line(cut, *self.terms), bit),)


def total_of(terms):
    rows = terms[-1].shape[0]
    return sum(term[:rows].astype(jnp.float32) for term in terms)


def tok_order(bits):
    order = [0]
    for bit in reversed(bits):
        order = order + [at | bit for at in order]
    return order


def kernel_params():
    return pltpu.CompilerParams(vmem_limit_bytes=VMEM_BYTES)


def kernel_cost(flops, *arrays):
    moved = sum(a.size * a.dtype.itemsize for a in arrays)
    return pl.CostEstimate(flops=flops, transcendentals=0, bytes_accessed=moved)


def any_space():
    return pl.BlockSpec(memory_space=pl.ANY)


def kept_block(shape):
    return pl.BlockSpec(shape, lambda *at: (0,) * len(shape), pipeline_mode=pl.Buffered(1))


def place(pieces, order, here):
    rows, width = pieces[0].shape[-2:]
    total = sum(p.shape[0] for p in pieces)

    def kernel(here_ref, *refs):
        *ins, out, held, arrive, leave = refs
        copies = []
        for mask, ref in zip(order, ins):
            for j in range(ref.shape[0]):
                at = len(copies)
                spot = j * len(order) + (here_ref[0] ^ mask)
                start = pl.multiple_of(spot * rows, rows)
                copies.append(
                    (
                        pltpu.make_async_copy(ref.at[j], held.at[at], arrive.at[at]),
                        pltpu.make_async_copy(
                            held.at[at], out.at[pl.ds(start, rows)], leave.at[at]
                        ),
                    )
                )
        for first, _ in copies:
            first.start()
        for first, then in copies:
            first.wait()
            then.start()
        for _, then in copies:
            then.wait()

    out = jax.ShapeDtypeStruct((total * rows, width), pieces[0].dtype)
    return pl.pallas_call(
        kernel,
        in_specs=[pl.BlockSpec(memory_space=pltpu.SMEM)] + [any_space()] * len(pieces),
        out_specs=any_space(),
        out_shape=out,
        scratch_shapes=[
            pltpu.VMEM((total, rows, width), pieces[0].dtype),
            pltpu.SemaphoreType.DMA((total,)),
            pltpu.SemaphoreType.DMA((total,)),
        ],
        compiler_params=kernel_params(),
        cost_estimate=kernel_cost(0, out, out),
    )(here, *pieces)


def over_pieces(pieces, which, extra, extra_specs, outs, compute, flops):
    rows, width = pieces[0].shape[-2:]
    total = rows * len(pieces)
    block = max(rows, min(512, total))
    each = block // rows

    def kernel(*refs):
        ins = refs[: len(pieces)]
        others = refs[len(pieces) : len(pieces) + len(extra)]
        results = refs[len(pieces) + len(extra) : -2]
        held, arrive = refs[-2:]
        step = pl.program_id(0)

        def copy(at, ref):
            return pltpu.make_async_copy(
                ref.at[which], held.at[pl.ds(at * rows, rows)], arrive.at[at]
            )

        @pl.when(step == 0)
        def start_all():
            for at, ref in enumerate(ins):
                copy(at, ref).start()

        for part in range(each):
            copy(step * each + part, ins[0]).wait()
        x = held[pl.ds(pl.multiple_of(step * block, block), block)]
        results[0][...] = x
        compute(x, others, results[1:])

    row_spec = lambda n: pl.BlockSpec((block, n), lambda i: (i, 0))
    shapes = [jax.ShapeDtypeStruct((total, n), jnp.bfloat16) for n in (width,) + tuple(outs)]
    return pl.pallas_call(
        kernel,
        grid=(total // block,),
        in_specs=[any_space()] * len(pieces) + [spec(row_spec) for spec in extra_specs],
        out_specs=[row_spec(s.shape[1]) for s in shapes],
        out_shape=shapes,
        scratch_shapes=[
            pltpu.VMEM((total, width), pieces[0].dtype),
            pltpu.SemaphoreType.DMA((len(pieces),)),
        ],
        compiler_params=kernel_params(),
        cost_estimate=kernel_cost(flops, *shapes, *extra),
    )(*pieces, *extra)


def feed_forward(pieces, which, weight):
    hidden = weight.shape[1] // 2
    total = len(pieces) * pieces[0].shape[-2]

    def compute(x, others, results):
        both = jnp.dot(x, others[0][...], preferred_element_type=jnp.float32)
        gate, up = (both[:, :hidden], both[:, hidden:])
        results[0][...] = both.astype(jnp.bfloat16)
        results[1][...] = (gate * jax.nn.sigmoid(gate) * up).astype(jnp.bfloat16)

    return over_pieces(
        pieces,
        which,
        (weight,),
        (lambda row_spec: kept_block(weight.shape),),
        (2 * hidden, hidden),
        compute,
        2 * total * weight.size,
    )


def feed_backward(pieces, which, weight, both):
    hidden = weight.shape[1]
    total = len(pieces) * pieces[0].shape[-2]

    def compute(x, others, results):
        grad = jnp.dot(x, others[0][...], preferred_element_type=jnp.float32)
        gate = others[1][:, :hidden].astype(jnp.float32)
        up = others[1][:, hidden:].astype(jnp.float32)
        sig = jax.nn.sigmoid(gate)
        results[0][:, :hidden] = (grad * up * sig * (1.0 + gate * (1.0 - sig))).astype(jnp.bfloat16)
        results[0][:, hidden:] = (grad * gate * sig).astype(jnp.bfloat16)

    return over_pieces(
        pieces,
        which,
        (weight, both),
        (lambda row_spec: kept_block(weight.shape), lambda row_spec: row_spec(2 * hidden)),
        (2 * hidden,),
        compute,
        2 * total * weight.size,
    )


def products_cut(lefts, weights, order):
    total, width = (lefts[0].shape[0], weights[0].shape[0])
    steps = order.shape[0]
    rows = total // steps
    half = steps // 2
    pairs = len(lefts)

    def kernel(order_ref, *refs):
        out = 0.0
        for left, weight in zip(refs[:pairs], refs[pairs : 2 * pairs]):
            out = out + lax.dot_general(
                left[...],
                weight[...],
                (((1,), (1,)), ((), ())),
                preferred_element_type=jnp.float32,
            )
        sent_ref, kept_ref = refs[2 * pairs :]
        step = pl.program_id(0)

        @pl.when(step < half)
        def first_part():
            sent_ref[...] = out.astype(jnp.bfloat16)

        @pl.when(step >= half)
        def second_part():
            kept_ref[...] = out.astype(jnp.bfloat16)

    part = jax.ShapeDtypeStruct((total // 2, width), jnp.bfloat16)
    sent, kept = pl.pallas_call(
        kernel,
        grid_spec=pltpu.PrefetchScalarGridSpec(
            num_scalar_prefetch=1,
            grid=(steps,),
            in_specs=[
                pl.BlockSpec(
                    (rows, left.shape[1]), lambda i, at: (at[lax.rem(i + half, steps)], 0)
                )
                for left in lefts
            ]
            + [kept_block(weight.shape) for weight in weights],
            out_specs=[
                pl.BlockSpec((rows, width), lambda i, at: (jnp.minimum(i, half - 1), 0)),
                pl.BlockSpec((rows, width), lambda i, at: (jnp.maximum(i - half, 0), 0)),
            ],
        ),
        out_shape=[part, part],
        compiler_params=kernel_params(),
        cost_estimate=kernel_cost(
            sum(2 * total * weight.size for weight in weights), part, part, *lefts, *weights
        ),
    )(order, *lefts, *weights)
    return (kept, sent)


def grad_product(rows_of, columns_of, which=None, far=None):
    sets = len(columns_of)
    count = len(rows_of)
    total, width = rows_of[0].shape
    columns = columns_of[0][0].shape[1]
    part, at = (columns, 0) if which is None else (columns // 2, which)
    block = 256
    narrow = part % 128 != 0

    def kernel(*refs):
        rows = refs[:count]
        for k in range(sets):
            out = 0.0
            for left, right in zip(rows, refs[count + k * count : count + (k + 1) * count]):
                right = right[:, at * part : (at + 1) * part] if narrow else right[...]
                out = out + lax.dot_general(
                    left[...],
                    right,
                    (((0,), (0,)), ((), ())),
                    preferred_element_type=jnp.float32,
                )
            cut = slice(k * part, (k + 1) * part)
            if far is not None:
                out = out + refs[-2][:, cut].astype(jnp.float32)
            refs[-1][:, cut] = out.astype(jnp.bfloat16)

    out = jax.ShapeDtypeStruct((width, sets * part), jnp.bfloat16)
    flat_columns = [c for columns_set in columns_of for c in columns_set]
    column_spec = pl.BlockSpec(
        (total, columns) if narrow else (total, part),
        lambda i: (0, 0 if narrow else at),
        pipeline_mode=pl.Buffered(1),
    )
    out_spec = pl.BlockSpec((block, sets * part), lambda i: (i, 0))
    extra = [] if far is None else [far]
    return pl.pallas_call(
        kernel,
        grid=(width // block,),
        in_specs=[pl.BlockSpec((total, block), lambda i: (0, i))] * count
        + [column_spec] * len(flat_columns)
        + [out_spec] * len(extra),
        out_specs=out_spec,
        out_shape=out,
        compiler_params=kernel_params(),
        cost_estimate=kernel_cost(
            2 * count * total * width * part * sets, out, *rows_of, *flat_columns
        ),
    )(*rows_of, *flat_columns, *extra)


def seg_send(value, counts, step):
    size = lax.axis_size("seg")
    packed = jnp.concatenate([value, counts], axis=1).astype(jnp.bfloat16)
    return [
        lax.ppermute(
            packed,
            "seg",
            [(k, k + step * far) for k in range(size) if 0 <= k + step * far < size],
        )
        for far in range(1, size)
    ]


def seg_sum(arrived):
    total = sum(part.astype(jnp.float32) for part in arrived)
    return (total[:, :-1], total[:, -1:])


def column_half(weight, which):
    half = weight.shape[1] // 2
    return lax.dynamic_slice_in_dim(weight, which * half, half, 1)


def seg_gather(value):
    return lax.all_gather(value, "seg", axis=0, tiled=True)


def other_segments(gathered):
    size, here = (lax.axis_size("seg"), lax.axis_index("seg"))
    rows = gathered.shape[0] // size
    return jnp.concatenate(
        [
            lax.dynamic_slice_in_dim(gathered, lax.rem(here + k, size) * rows, rows, 0)
            for k in range(1, size)
        ],
        axis=0,
    )


def with_other(mine, got, own, pieces):
    size = mine.shape[0] // own.shape[0]
    rows, half = (own.shape[0], own.shape[1] // pieces)
    here = lax.axis_index("seg").astype(jnp.int32)[None]

    def kernel(here_ref, mine_ref, got_ref, own_ref, *outs):
        is_own = pl.program_id(0) == here_ref[0]
        rest = jnp.where(is_own, own_ref[...], got_ref[...])
        for k, out in enumerate(outs):
            cut = slice(k * half, (k + 1) * half)
            out[:, :half] = mine_ref[:, cut]
            out[:, half:] = rest[:, cut]

    def got_block(i, at):
        return (jnp.minimum(lax.rem(i + size - at[0] - 1 + size, size), size - 2), 0)

    out = jax.ShapeDtypeStruct((mine.shape[0], 2 * half), mine.dtype)
    return pl.pallas_call(
        kernel,
        grid_spec=pltpu.PrefetchScalarGridSpec(
            num_scalar_prefetch=1,
            grid=(size,),
            in_specs=[
                pl.BlockSpec((rows, own.shape[1]), lambda i, at: (i, 0)),
                pl.BlockSpec((rows, own.shape[1]), got_block),
                pl.BlockSpec((rows, own.shape[1]), lambda i, at: (0, 0)),
            ],
            out_specs=[pl.BlockSpec((rows, 2 * half), lambda i, at: (i, 0))] * pieces,
        ),
        out_shape=[out] * pieces,
        compiler_params=kernel_params(),
        cost_estimate=kernel_cost(0, mine, mine, mine, mine),
    )(here, mine, got, own)


def seg_scatter(value):
    return lax.psum_scatter(value, "seg", scatter_dimension=0, tiled=True)


def whole_columns(own, rest):
    first = lax.axis_index("grp") == 0
    return jnp.where(
        first, jnp.concatenate([own, rest], axis=1), jnp.concatenate([rest, own], axis=1)
    ).astype(jnp.float32)


def whole_sum(own, far):
    half = own.shape[1] // 2
    turned = jnp.concatenate([far[:, half:], far[:, :half]], axis=1)
    total = added(own, turned)
    first = lax.axis_index("grp") == 0
    return jnp.where(first, total, jnp.concatenate([total[:, half:], total[:, :half]], axis=1))


def times(left, right):
    return jnp.dot(left, right, preferred_element_type=jnp.float32)


def times_rows(left, right):
    return jnp.einsum("tc,dc->td", left, right, preferred_element_type=jnp.float32)


def weight_grad(rows, columns):
    return jnp.einsum("td,tc->dc", rows, columns, preferred_element_type=jnp.float32)


def root_norm(values, gain):
    return values * lax.rsqrt(jnp.mean(values * values, -1, keepdims=True) + EPS_NORM) * gain


def positive_feature(values):
    return jnp.where(values > 0, values + 1.0, jnp.exp(jnp.where(values > 0, 0.0, values)))


def feature_slope(values):
    return jnp.where(values > 0, 1.0, jnp.exp(jnp.where(values > 0, 0.0, values)))


def dot_as(left, right, dims):
    return lax.dot_general(left, right, (dims, ((), ())), preferred_element_type=jnp.float32)


ROWS_COLUMNS = ((1,), (0,))
BY_COLUMNS = ((1,), (1,))
BY_ROWS = ((0,), (0,))


def head_call(kernel, ins, outs, flops, scratch=()):
    def spec(shape, kind):
        if kind == "smem":
            return pl.BlockSpec(memory_space=pltpu.SMEM)
        if kind == "all":
            return kept_block(shape)
        if kind == "columns":
            return pl.BlockSpec((shape[0], HEAD_DIM), lambda i: (0, i))
        return pl.BlockSpec((1,) + shape[1:], lambda i: (i, 0, 0))

    heads = [s.shape[0] for s, kind in outs if kind == "heads"] + [
        s.shape[1] // HEAD_DIM for s, kind in outs if kind == "columns"
    ]
    return pl.pallas_call(
        kernel,
        grid=(heads[0],),
        in_specs=[spec(a.shape, kind) for a, kind in ins],
        out_specs=[spec(s.shape, kind) for s, kind in outs],
        out_shape=[s for s, kind in outs],
        scratch_shapes=list(scratch),
        compiler_params=kernel_params(),
        cost_estimate=kernel_cost(
            flops, *[a for a, kind in ins if kind != "smem"], *[s for s, kind in outs]
        ),
    )(*[a for a, kind in ins])


def low_feature(values):
    return positive_feature(values.astype(jnp.float32)).astype(jnp.bfloat16)


def like(shape, dtype):
    return jax.ShapeDtypeStruct(shape, dtype)


def features(key_rows, values):
    heads = key_rows.shape[1] // HEAD_DIM

    def kernel(key_ref, value_ref, contrib_ref, count_ref):
        feat_k = low_feature(key_ref[...])
        contrib_ref[0] = dot_as(feat_k, value_ref[...], BY_ROWS)
        count_ref[0] = jnp.sum(feat_k.astype(jnp.float32), axis=0, keepdims=True)

    return head_call(
        kernel,
        [(key_rows, "columns"), (values, "columns")],
        [
            (like((heads, HEAD_DIM, HEAD_DIM), jnp.float32), "heads"),
            (like((heads, 1, HEAD_DIM), jnp.float32), "heads"),
        ],
        2 * SEG_LEN * heads * HEAD_DIM**2,
    )


def reach_of(at):
    return min(SEG_LEN, (at + 2) * PIECE)


def masked_scores(query_block, keys, at, piece_first):
    scores = dot_as(query_block, keys, BY_COLUMNS) * HEAD_DIM ** (-0.5)
    rows_at = at * PIECE + lax.broadcasted_iota(jnp.int32, scores.shape, 0)
    keys_at = lax.broadcasted_iota(jnp.int32, scores.shape, 1)
    row_in = (rows_at >= piece_first) & (rows_at < piece_first + PIECE)
    key_in = (keys_at >= piece_first) & (keys_at < piece_first + PIECE)
    return jnp.where((keys_at <= rows_at) | (row_in & key_in), scores, MASKED_SCORE)


def local_flops(heads, products):
    return products * 2 * heads * HEAD_DIM * PIECE * sum(reach_of(k) for k in range(SEG_LEN // PIECE))


def local_attention(queries, key_rows, values, piece_first):
    heads = queries.shape[1] // HEAD_DIM

    def kernel(first_ref, query_ref, key_ref, value_ref, out_ref, log_ref):
        first = first_ref[0]
        for at in range(SEG_LEN // PIECE):
            rows = slice(at * PIECE, (at + 1) * PIECE)
            reach = reach_of(at)
            scores = masked_scores(query_ref[rows, :], key_ref[:reach, :], at, first)
            peak = jnp.max(scores, axis=-1, keepdims=True)
            shifted = jnp.exp(scores - peak)
            total = jnp.sum(shifted, axis=-1, keepdims=True)
            probs = (shifted * (1.0 / total)).astype(jnp.bfloat16)
            out_ref[rows, :] = dot_as(probs, value_ref[:reach, :], ROWS_COLUMNS)
            log_ref[0, rows, :] = peak + jnp.log(total)

    return head_call(
        kernel,
        [
            (piece_first[None], "smem"),
            (queries, "columns"),
            (key_rows, "columns"),
            (values, "columns"),
        ],
        [
            (like(queries.shape, jnp.float32), "columns"),
            (like((heads, SEG_LEN, 1), jnp.float32), "heads"),
        ],
        local_flops(heads, 2),
    )


def recalled(feat_q, memory, norm_mem):
    numerator = dot_as(feat_q, memory.astype(jnp.bfloat16), ROWS_COLUMNS)
    denominator = 1.0 + jnp.sum(feat_q.astype(jnp.float32) * norm_mem, axis=-1, keepdims=True)
    return (numerator / denominator, denominator)


def mixing(queries, local_out, memory, norm_mem, share):
    heads = queries.shape[1] // HEAD_DIM

    def kernel(share_ref, query_ref, local_ref, memory_ref, norm_ref, out_ref):
        part = share_ref[pl.program_id(0)]
        recall, unused = recalled(low_feature(query_ref[...]), memory_ref[0], norm_ref[0])
        out_ref[...] = (part * recall + (1.0 - part) * local_ref[...]).astype(jnp.bfloat16)

    return head_call(
        kernel,
        [
            (share, "smem"),
            (queries, "columns"),
            (local_out, "columns"),
            (memory, "heads"),
            (norm_mem, "heads"),
        ],
        [(like(queries.shape, jnp.bfloat16), "columns")],
        2 * SEG_LEN * heads * HEAD_DIM**2,
    )[0]


def memory_backward(grad_att, out_full, queries, local_out, memory, norm_mem, share):
    heads = queries.shape[1] // HEAD_DIM

    def kernel(
        share_ref,
        grad_ref,
        weight_ref,
        query_ref,
        local_ref,
        memory_ref,
        norm_ref,
        logit_ref,
        grad_local_ref,
        grad_query_ref,
        grad_memory_ref,
        grad_norm_ref,
    ):
        part = share_ref[pl.program_id(0)]
        queries_f = query_ref[...].astype(jnp.float32)
        feat_q = low_feature(query_ref[...])
        recall, denominator = recalled(feat_q, memory_ref[0], norm_ref[0])
        grad_mixed = dot_as(grad_ref[...], weight_ref[...], ROWS_COLUMNS)
        logit_ref[0] = jnp.sum(grad_mixed * (recall - local_ref[...]), axis=0, keepdims=True)
        grad_local_ref[...] = ((1.0 - part) * grad_mixed).astype(jnp.bfloat16)
        grad_scaled = part * grad_mixed / denominator
        grad_numer = grad_scaled.astype(jnp.bfloat16)
        grad_denom = -jnp.sum(grad_scaled * recall, axis=-1, keepdims=True)
        grad_feat = (
            dot_as(grad_numer, memory_ref[0].astype(jnp.bfloat16), BY_COLUMNS)
            + grad_denom * norm_ref[0]
        )
        grad_query_ref[...] = grad_feat * feature_slope(queries_f)
        grad_memory_ref[0] = dot_as(feat_q, grad_numer, BY_ROWS)
        grad_norm_ref[0] = jnp.sum(feat_q.astype(jnp.float32) * grad_denom, axis=0, keepdims=True)

    square = like((heads, HEAD_DIM, HEAD_DIM), jnp.float32)
    row = like((heads, 1, HEAD_DIM), jnp.float32)
    return head_call(
        kernel,
        [
            (share, "smem"),
            (grad_att, "all"),
            (out_full, "columns"),
            (queries, "columns"),
            (local_out, "columns"),
            (memory, "heads"),
            (norm_mem, "heads"),
        ],
        [
            (row, "heads"),
            (like(queries.shape, jnp.bfloat16), "columns"),
            (like(queries.shape, jnp.float32), "columns"),
            (square, "heads"),
            (row, "heads"),
        ],
        2 * grad_att.size * queries.shape[1] + 6 * SEG_LEN * heads * HEAD_DIM**2,
    )


def local_backward(queries, key_rows, values, log_totals, grad_local, grad_query, piece_first):
    heads = queries.shape[1] // HEAD_DIM

    def kernel(
        first_ref,
        query_ref,
        key_ref,
        value_ref,
        log_ref,
        local_ref,
        memory_ref,
        query_out,
        key_out,
        value_out,
    ):
        first = first_ref[0]
        scale = HEAD_DIM ** (-0.5)
        for at in range(SEG_LEN // PIECE):
            rows = slice(at * PIECE, (at + 1) * PIECE)
            reach = reach_of(at)
            known = reach_of(at - 1) if at > 0 else 0
            query_block = query_ref[rows, :]
            local_block = local_ref[rows, :]
            scores = masked_scores(query_block, key_ref[:reach, :], at, first)
            probs = jnp.exp(scores - log_ref[0, rows, :])
            grad_probs = dot_as(local_block, value_ref[:reach, :], BY_COLUMNS)
            weighed = probs * grad_probs
            mean = jnp.sum(weighed, axis=-1, keepdims=True)
            grad_scores = (weighed - probs * mean).astype(jnp.bfloat16)
            query_out[rows, :] = (
                dot_as(grad_scores, key_ref[:reach, :], ROWS_COLUMNS) * scale + memory_ref[rows, :]
            ).astype(jnp.bfloat16)
            for out, part in (
                (key_out, dot_as(grad_scores, query_block, BY_ROWS) * scale),
                (value_out, dot_as(probs.astype(jnp.bfloat16), local_block, BY_ROWS)),
            ):
                if known > 0:
                    out[:known, :] += part[:known]
                if known < reach:
                    out[known:reach, :] = part[known:]

    wide = (like(queries.shape, jnp.float32), "columns")
    return head_call(
        kernel,
        [
            (piece_first[None], "smem"),
            (queries, "columns"),
            (key_rows, "columns"),
            (values, "columns"),
            (log_totals, "heads"),
            (grad_local, "columns"),
            (grad_query, "columns"),
        ],
        [(like(queries.shape, jnp.bfloat16), "columns"), wide, wide],
        local_flops(heads, 5),
    )


def with_memory(key_rows, values, key_sum, value_sum, grad_contrib, grad_count):
    heads = key_rows.shape[1] // HEAD_DIM

    def kernel(key_ref, value_ref, key_sum, value_sum, contrib_ref, count_ref, key_out, value_out):
        keys = key_ref[...]
        contrib = contrib_ref[0].astype(jnp.bfloat16)
        grad_feat = dot_as(value_ref[...], contrib, BY_COLUMNS) + count_ref[0]
        slope = feature_slope(keys.astype(jnp.float32))
        key_out[...] = (key_sum[...] + grad_feat * slope).astype(jnp.bfloat16)
        value_out[...] = (
            value_sum[...] + dot_as(low_feature(keys), contrib, ROWS_COLUMNS)
        ).astype(jnp.bfloat16)

    out = (like(key_rows.shape, jnp.bfloat16), "columns")
    return head_call(
        kernel,
        [
            (key_rows, "columns"),
            (values, "columns"),
            (key_sum, "columns"),
            (value_sum, "columns"),
            (grad_contrib, "heads"),
            (grad_count, "heads"),
        ],
        [out, out],
        4 * SEG_LEN * heads * HEAD_DIM**2,
    )


def body(
    hidden_in,
    cotangent,
    piece_start,
    query_weight,
    key_weight,
    value_weight,
    out_weight,
    gate_weight,
    up_weight,
    down_weight,
    attend_gain,
    feed_gain,
    gate_logit,
):
    line = Line(attend_gain)
    group = lax.axis_index("grp")
    count, rows, width = hidden_in.shape
    micros = range(count)
    columns = query_weight.shape[1]
    half = columns // 2
    head_local = columns // HEAD_DIM
    head_turn = group * (head_local // 2)
    heads_here = lax.axis_index("tok") * head_local + lax.rem(
        jnp.arange(head_local, dtype=jnp.int32) + head_turn, head_local
    )
    placement = (
        jnp.arange(HEADS, dtype=jnp.int32)[None, :] == heads_here[:, None]
    ).astype(jnp.float32)
    gate_local = jnp.sum(placement * gate_logit[None, :], axis=1)
    share = jax.nn.sigmoid(gate_local)
    piece_first = [piece_start[m, 0] - lax.axis_index("seg") * SEG_LEN for m in micros]

    def halves(*weights):
        return jnp.concatenate([column_half(w, group) for w in weights], axis=1)

    def other_halves(*weights):
        return jnp.concatenate([column_half(w, 1 - group) for w in weights], axis=1)

    bits = tok_bits()
    here = lax.axis_index("tok")
    order = tok_order(bits)
    here = here.astype(jnp.int32)[None]
    spots = jnp.array(order, jnp.int32) ^ here
    in_turn = jnp.arange(2 * len(order), dtype=jnp.int32)

    pair_weights = (query_weight, key_weight)
    pair_mine = seg_gather(line(halves, *pair_weights))
    normed_a = line(
        lambda x: root_norm(x.astype(jnp.float32), attend_gain).astype(jnp.bfloat16), hidden_in
    )
    attend_pieces = FirstPiece(normed_a, bits)
    cot_swapped = grp_swap(cotangent)
    value_mine = seg_gather(line(halves, value_weight))
    out_mine = seg_gather(line(halves, out_weight))
    feed_mine = seg_gather(line(halves, gate_weight, up_weight))
    down_mine = seg_gather(line(halves, down_weight))
    pair_other = line(other_halves, *pair_weights)
    value_other = line(other_halves, value_weight)
    out_other = line(other_halves, out_weight)
    cot_swapped = line.hold(cot_swapped)
    attend_pieces = attend_pieces.rest(line)
    cot_pieces = FirstPiece(line.hold(cotangent), bits)
    pair_got = grp_swap(line(other_segments, pair_mine))
    gathered_a = line(
        lambda *p: place(p, order, here),
        *[attend_pieces[at] for at in order],
    )
    gathered_a = [gathered_a[m * SEG_LEN : (m + 1) * SEG_LEN] for m in micros]
    value_got = grp_swap(line(other_segments, value_mine))

    def project(g, *weights):
        return tuple(
            tuple(times(g[m], w).astype(jnp.bfloat16) for m in micros) for w in weights
        )

    query_full, key_full = line(lambda *a: with_other(*a, 2), pair_mine, pair_got, pair_other)
    queries, key_rows = line(project, gathered_a, query_full, key_full)
    cot_pieces = cot_pieces.rest(line)
    cot_far = FirstPiece(cot_swapped, bits)
    (value_full,) = line(lambda *a: with_other(*a, 1), value_mine, value_got, value_other)
    (values,) = line(project, gathered_a, value_full)
    out_got = grp_swap(line(other_segments, out_mine))

    contrib, count_k = zip(*[line(features, key_rows[m], values[m]) for m in micros])
    arrived = seg_send(jnp.concatenate(contrib), jnp.concatenate(count_k), 1)
    local = [line(local_attention, queries[0], key_rows[0], values[0], piece_first[0])]
    (out_full,) = line(lambda *a: with_other(*a, 1), out_mine, out_got, out_other)
    cot_far = cot_far.rest(line)
    memory, norm_mem = line(seg_sum, arrived)
    memory = [memory[m * head_local : (m + 1) * head_local] for m in micros]
    norm_mem = [norm_mem[m * head_local : (m + 1) * head_local] for m in micros]
    mixes = []
    attended = []

    def mixed_rows(m):
        mixes.append(line(mixing, queries[m], local[m][0], memory[m], norm_mem[m], share))
        return line(lambda a, w: products_cut([a], [w], spots), mixes[m], out_full)

    for m in micros:
        if m > 0:
            local.append(line(local_attention, queries[m], key_rows[m], values[m], piece_first[m]))
        cut = mixed_rows(m)
        if m > 0:
            cut, attended[m - 1].terms = line.hold((cut, attended[m - 1].terms))
        attended.append(Scatter(*cut))
        attended[m].go_on(line)

    def after_attention(x, terms):
        resid = x.astype(jnp.float32) + total_of(terms)
        return (resid, root_norm(resid, feed_gain).astype(jnp.bfloat16))

    resid = []
    feed_pieces = []
    for m in micros:
        rows_m, normed_f = line(after_attention, hidden_in[m], attended[m].terms)
        resid.append(rows_m)
        over_tok = None
        if m + 1 < count:
            over_tok, attended[m + 1].terms = line.hold((normed_f[None], attended[m + 1].terms))
        feed_pieces.append(BothGroups(normed_f[None], bits, over_tok))
    for pieces in feed_pieces:
        pieces.go_on(line)
    feed_mine = line.hold(feed_mine)

    def interleaved(own, far):
        return [pieces[at] for at in order for pieces in (own, far)]

    feed_in = []
    products = []
    inner_act = []
    for m in micros:
        rows_m, both, inner = line(
            lambda w, *p: feed_forward(p, 0, w), feed_mine, *interleaved(*feed_pieces[m].finish(line))
        )
        feed_in.append(rows_m)
        products.append(both)
        inner_act.append(inner)

    cot_all = []
    grad_products = []
    grad_normed = []

    def backward(m):
        rows_m, grads = line(
            lambda w, both, *p: feed_backward(p, m, w, both),
            down_mine,
            products[m],
            *interleaved(cot_pieces, cot_far),
        )
        cot_all.append(rows_m)
        grad_products.append(grads)

    def backward_rows(m):
        return line(lambda a, w: products_cut([a], [w], in_turn), grad_products[m], feed_mine)

    def own_and_far(terms):
        total = total_of(terms)
        half = total.shape[0] // 2
        return (total[:half], total[half:].astype(jnp.bfloat16))

    def after_feed_grad(rows_m, own, far, cot):
        unused_norm, pull = jax.vjp(root_norm, rows_m, feed_gain)
        grad_norm, gain_part = pull(added(own, far))
        grad_resid = cot.astype(jnp.float32) + grad_norm
        return (grad_resid, gain_part, grad_resid.astype(jnp.bfloat16))

    grad_parts = []
    grad_resid = []
    feed_gain_parts = []
    att_pieces = []

    def finish_rows(m):
        own, far = line(own_and_far, grad_normed[m].terms)
        grad_parts.append((own, grp_swap(far)))

    def finish_feed(m):
        rows_m, gain_part, low = line(after_feed_grad, resid[m], *grad_parts[m], cotangent[m])
        grad_resid.append(rows_m)
        feed_gain_parts.append(gain_part)
        att_pieces.append(FirstPiece(low[None], bits))

    feed_out = []

    def feed_result(m):
        return line(lambda a, w: products_cut([a], [w], in_turn), inner_act[m], down_mine)

    backward(0)
    grad_normed.append(Scatter(*backward_rows(0)))
    backward(1)
    grad_normed[0].go_on(line)
    down_raw = line(lambda a, b: grad_product(a, [b]), cot_all, inner_act)
    cut = backward_rows(1)
    down_raw, cut, grad_normed[0].terms = line.hold((down_raw, cut, grad_normed[0].terms))
    grad_normed.append(Scatter(*cut))
    down_grad = seg_scatter(down_raw)
    finish_rows(0)
    grad_normed[1].go_on(line)
    feed_raw = line(lambda a, b: grad_product(a, [b]), feed_in, grad_products)
    feed_raw, grad_normed[1].terms, grad_parts[0] = line.hold(
        (feed_raw, grad_normed[1].terms, grad_parts[0])
    )
    feed_grad = seg_scatter(feed_raw)
    finish_rows(1)
    finish_feed(0)
    cut = feed_result(0)
    cut, grad_parts[1], att_pieces[0].got = line.hold((cut, grad_parts[1], att_pieces[0].got))
    finish_feed(1)
    att_pieces[0] = att_pieces[0].rest(line)
    feed_out.append(Scatter(*cut))
    down_grad = line.hold(down_grad)
    down_rest = grp_swap(down_grad)

    grad_att = []
    mem_back = []
    for m in micros:
        if m > 0:
            feed_out[m - 1].go_on(line)
            cut = feed_result(m)
            att_pieces[m] = att_pieces[m].rest(line)
            feed_out.append(Scatter(*line.hold(cut)))
        grad_att.append(
            line(lambda *p: place(p, order, here), *[att_pieces[m][at] for at in order])
        )
        mem_back.append(
            line(
                memory_backward,
                grad_att[m],
                out_full,
                queries[m],
                local[m][0],
                memory[m],
                norm_mem[m],
                share,
            )
        )
    logit_parts, grad_local, grad_query, grad_memory, grad_norm_mem = zip(*mem_back)
    back_arrived = seg_send(jnp.concatenate(grad_memory), jnp.concatenate(grad_norm_mem), -1)
    out_far = grp_swap(line(lambda a, b: grad_product(a, [b], 1), grad_att, mixes))
    feed_out[-1].go_on(line)
    local_back = []

    def local_grad(m):
        local_back.append(
            line(
                local_backward,
                queries[m],
                key_rows[m],
                values[m],
                local[m][1],
                grad_local[m],
                grad_query[m],
                piece_first[m],
            )
        )

    local_grad(0)
    out_far = line.hold(out_far)
    down_out = line(whole_columns, down_grad, down_rest)
    local_grad(1)
    query_low, key_sums, value_sums = zip(*local_back)
    feed_parts = []
    for m in micros:
        own, far = line(own_and_far, feed_out[m].terms)
        feed_parts.append((own, grp_swap(far)))
    query_raw = line(lambda a, b: grad_product(a, [b]), gathered_a, query_low)
    feed_parts[0], grad_contrib, grad_count = line.hold(
        (feed_parts[0],) + line(seg_sum, back_arrived)
    )
    out_raw = line(lambda a, b, far: grad_product(a, [b], 0, far), grad_att, mixes, out_far)
    feed_grad, out_raw = line.hold((feed_grad, out_raw))
    feed_half = gate_weight.shape[1] // 2
    gate_grad, up_grad = (feed_grad[:, :feed_half], feed_grad[:, feed_half:])
    gate_rest = grp_swap(gate_grad)
    out_grad = seg_scatter(out_raw)
    key_low, value_low = zip(
        *[
            line(
                with_memory,
                key_rows[m],
                values[m],
                key_sums[m],
                value_sums[m],
                grad_contrib[m * head_local : (m + 1) * head_local],
                grad_count[m * head_local : (m + 1) * head_local],
            )
            for m in micros
        ]
    )
    pair_far = line(lambda a, c, d: grad_product(a, [c, d], 1), gathered_a, key_low, value_low)
    pair_far, gate_rest = line.hold((pair_far, gate_rest))
    pair_far = grp_swap(pair_far)
    query_sum = seg_scatter(query_raw)
    grad_normed_a = []
    for m in micros:
        grad_normed_a.append(
            Scatter(
                *line(
                    lambda a, b, c, wa, wb, wc: products_cut([a, b, c], [wa, wb, wc], spots),
                    query_low[m],
                    key_low[m],
                    value_low[m],
                    query_full,
                    key_full,
                    value_full,
                )
            )
        )
    pair_far, out_grad = line.hold((pair_far, out_grad))
    pair_raw = line(
        lambda far, a, c, d: grad_product(a, [c, d], 0, far),
        pair_far,
        gathered_a,
        key_low,
        value_low,
    )
    pair_grad = seg_scatter(pair_raw)
    up_rest = grp_swap(line.hold(up_grad))
    out_rest = grp_swap(out_grad)
    for m in micros:
        grad_normed_a[m].go_on(line)
    gate_out = line(whole_columns, gate_grad, gate_rest)

    def after_attend_grad(x, terms, grad, gain):
        unused_norm, pull = jax.vjp(root_norm, x.astype(jnp.float32), gain)
        grad_norm, gain_part = pull(total_of(terms))
        return ((grad + grad_norm).astype(jnp.bfloat16), gain_part)

    gain, line.token = (line.token, out_grad)
    input_rows = []
    attend_gain_parts = []
    for m in micros:
        grad_rows, gain_part = line(
            after_attend_grad, hidden_in[m], grad_normed_a[m].terms, grad_resid[m], gain
        )
        input_rows.append(grad_rows)
        attend_gain_parts.append(gain_part)
    feed_parts = line.hold(feed_parts)
    gate_logit_part = jnp.sum(sum(logit_parts), axis=(1, 2)) * share * (1.0 - share)
    gate_full_grad = jnp.sum(placement * gate_logit_part[:, None], axis=0)
    small = line(
        lambda a, b, c: jnp.concatenate([sum(a), sum(b), c])[None],
        attend_gain_parts,
        feed_gain_parts,
        gate_full_grad,
    )
    small_steps = [
        (axis, 1 << k)
        for axis in ("tok", "seg", "grp")
        for k in range(lax.axis_size(axis).bit_length() - 1)
    ]

    def add_small(small, axis, bit):
        size = lax.axis_size(axis)
        other = lax.ppermute(small, axis, [(k, k ^ bit) for k in range(size)])
        return line(jnp.add, small, other)

    for axis, bit in small_steps[:-3]:
        small = add_small(small, axis, bit)
    query_sum = line.hold(query_sum)
    query_rest = grp_swap(query_sum)
    pair_grad, small = line.hold((pair_grad, small))
    pair_rest = grp_swap(pair_grad)
    up_out = line(whole_columns, up_grad, up_rest)
    output_rows = [
        line(
            lambda r, own, far: (r + added(own, far)).astype(jnp.bfloat16), resid[m], *feed_parts[m]
        )
        for m in micros
    ]
    small = add_small(line.hold(small), *small_steps[-3])
    small = add_small(small, *small_steps[-2])
    query_grad = line(whole_sum, query_sum, query_rest)
    small = add_small(small, *small_steps[-1])
    key_grad, value_grad = line(
        lambda a, b: tuple(
            whole_columns(*[part[:, k * half : (k + 1) * half] for part in (a, b)])
            for k in range(2)
        ),
        pair_grad,
        pair_rest,
    )
    out_out = whole_columns(line.token, out_rest)
    small_sums = (small[0, :width], small[0, width : 2 * width], small[0, 2 * width :])
    return (
        (jnp.stack(output_rows), jnp.stack(input_rows))
        + (query_grad, key_grad, value_grad)
        + (out_out, gate_out, up_out, down_out)
        + small_sums
    )


def solution(mesh):
    return jax.shard_map(
        body,
        mesh=mesh,
        in_specs=(
            P("grp", ("seg", "tok"), None),
            P("grp", ("seg", "tok"), None),
            P("grp", "seg"),
            P("seg", "tok"),
            P("seg", "tok"),
            P("seg", "tok"),
            P("seg", "tok"),
            P("seg", "tok"),
            P("seg", "tok"),
            P("seg", "tok"),
            P(),
            P(),
            P(),
        ),
        out_specs=(
            P("grp", ("seg", "tok"), None),
            P("grp", ("seg", "tok"), None),
            P("seg", "tok"),
            P("seg", "tok"),
            P("seg", "tok"),
            P("seg", "tok"),
            P("seg", "tok"),
            P("seg", "tok"),
            P("seg", "tok"),
            P(),
            P(),
            P(),
        ),
        check_vma=False,
    )
```
